128 devices in a mesh: row: 32 (over z_lo, x, y), col: 4 (over z_hi, core).
Axes of the slice: x: 4, y: 4, z: 4 (z_hi: 2, z_lo: 2; z = z_hi * 2 + z_lo), core: 2. Of those that a mesh axis runs over, the one named last changes fastest.
Arguments:
- amplitudes: bfloat16 [1024, 28672], P(('row', 'col')), may hold values from -6 to 6
- amplitude_mask: int32 [1024, 224], P(('row', 'col')), may hold values 0 or 1
- integrals: bfloat16 [28672, 28672], P('row', 'col'), may hold values from -0.03125 to 0.03125
- integral_mask: int32 [224, 224], P('row', 'col'), may hold values from 0 to 1, as said below
- tile_order: int32 [224], replicated, may hold values from 0 to 223, each once
Outputs:
- ladder: bfloat16 [1024, 28672], P(('row', 'col'))
The draws below stay inside these ranges and needn't reach their ends.
Inputs may be any that keep to these rules, and one draw needn't show every extreme that they name: `amplitude_mask`: 1 keeps a tile of amplitudes, 0 drops it. `integral_mask`: 1 keeps a tile of integrals, 0 drops it. `tile_order`: each tile of 0 to 223 appears once.
All inputs are finite; a program needn't handle non-finite values. No bound on the sum of `amplitude_mask` on one device may be relied on, other than what follows from the above.
Results may differ from the reference program's by a relative error of at most 0.0012.
Values may be sent and summed in bfloat16 or wider, within the bound.
No kernel may reach another device: no remote copies, remote signals or barrier semaphores. Data moves between devices by JAX's collectives and lax.ppermute only.
A program may use at most 128 MiB of HBM per device.

```python
import jax
import jax.numpy as jnp
from jax import lax

QT = 224
Q = 28672
P_SIZE = 1024
N_ROW = 32


def draw_integral_mask(key, part):
    key = jax.random.fold_in(key, 7)
    first_key, second_key = jax.random.split(key)
    density = jax.random.randint(first_key, (QT, 1), 2, 10)
    levels = jax.random.randint(second_key, (QT, QT), 0, 10)
    return (levels < density).astype(jnp.int32)


def with_ends(values, rng, least, largest):
    index_at = [jax.random.randint(jax.random.fold_in(rng, axis), (), 0, length) for axis, length in enumerate(values.shape)]
    longest = values.shape.index(max(values.shape))
    beside = index_at[:longest] + [(index_at[longest] + 1) % values.shape[longest]] + index_at[longest + 1:]
    return values.at[tuple(index_at)].set(least).at[tuple(beside)].set(largest)


def level_of(key, dims, cuts, least, top_value):
    loudness = 1.0
    for position, shards_of in cuts:
        draws = jax.random.uniform(jax.random.fold_in(jax.random.fold_in(key, 6), position), (shards_of,), jnp.float32, least / len(cuts), top_value / len(cuts))
        loudness = loudness * jnp.repeat(jnp.exp(draws), dims[position] // shards_of).reshape((-1,) + (1,) * (len(dims) - 1 - position))
    return loudness


def gaussian(rng, shape, deviation, bound, cuts=(), kind=jnp.bfloat16):
    factor_of = level_of(rng, shape, cuts, -0.22, 0.18) if cuts else 1.0
    values = jax.random.normal(rng, shape, jnp.float32) * deviation * factor_of
    return jnp.minimum(jnp.maximum(values, -bound), bound).astype(kind)


def setup_inputs(seed: int = 0) -> dict:
    splits = jax.random.split(jax.random.key(seed), 6)
    amplitudes = gaussian(splits[0], (P_SIZE, Q), 1.0, 6.0, ((0, 128),))
    amplitude_mask = with_ends((jax.random.randint(splits[1], (P_SIZE, QT), 0, 3) < 2).astype(jnp.int32), jax.random.fold_in(splits[1], 1), 0, 1)
    integrals = gaussian(splits[2], (Q, Q), Q ** -0.5, 0.03125, ((0, 32), (1, 4)))
    integral_mask = draw_integral_mask(jax.random.fold_in(splits[5], 71), 0)
    tile_order = jax.random.permutation(splits[4], QT).astype(jnp.int32)
    return {"amplitudes": amplitudes, "amplitude_mask": amplitude_mask, "integrals": integrals, "integral_mask": integral_mask, "tile_order": tile_order}


def mask_block(block_values, flag_tiles):
    row_count, col_count = block_values.shape
    row_tiles, col_tiles = flag_tiles.shape
    shaped = block_values.reshape(row_tiles, row_count // row_tiles, col_tiles, col_count // col_tiles)
    return (shaped * flag_tiles.astype(jnp.bfloat16)[:, None, :, None]).reshape(row_count, col_count)


def reference(amplitudes, amplitude_mask, integrals, integral_mask, tile_order):
    pair_count, full_width = amplitudes.shape
    tile_count = amplitude_mask.shape[1]
    shaped = amplitudes.reshape(pair_count, tile_count, full_width // tile_count) * amplitude_mask.astype(jnp.bfloat16)[:, :, None]
    ordered = jnp.take(shaped, tile_order, axis=1).reshape(pair_count, full_width).astype(jnp.float32)
    block_rows = full_width // N_ROW
    row_tiles = tile_count // N_ROW

    def accumulate(block_index, running):
        begin_row = (block_index * block_rows).astype(jnp.int32)
        begin_tile = (block_index * row_tiles).astype(jnp.int32)
        left_part = lax.dynamic_slice_in_dim(ordered, begin_row, block_rows, 1)
        block_values = lax.dynamic_slice_in_dim(integrals, begin_row, block_rows, 0)
        flag_tiles = lax.dynamic_slice_in_dim(integral_mask, begin_tile, row_tiles, 0)
        right_part = mask_block(block_values, flag_tiles).astype(jnp.float32)
        block_term = jnp.dot(left_part, right_part, precision=lax.Precision.HIGHEST, preferred_element_type=jnp.float32)
        return running + block_term

    running = lax.fori_loop(0, N_ROW, accumulate, jnp.zeros((pair_count, full_width), jnp.float32))
    return running.astype(jnp.bfloat16)
```

```python
import functools

import jax
import jax.numpy as jnp
from jax import lax
from jax.experimental import pallas as pl
from jax.experimental.pallas import tpu as pltpu
from jax.sharding import PartitionSpec as P

N_CHUNK = 2
TILE = 256
LEVELS = 32600.0
STEPS = 32.0
VMEM_LIMIT = 48 * 1024 * 1024


def shift(dz, dx, dy):
    pairs = []
    for index in range(32):
        z, x, y = index // 16, (index // 4) % 4, index % 4
        pairs.append((index, ((z + dz) % 2) * 16 + ((x + dx) % 4) * 4 + (y + dy) % 4))
    return pairs


FORWARD = (shift(0, 1, 0), shift(0, 0, 1))
BACKWARD = (shift(0, -1, 0), shift(0, 0, -1))
ACROSS = shift(1, 0, 0)


def send(value, pairs):
    return lax.ppermute(value, "row", pairs)


def left_rows(a_ref, kind, first):
    first_stride, second_stride = (128, 32) if kind == 0 else (32, 128)
    blocks = []
    for z in range(2):
        for second in range(4):
            start = pl.multiple_of(z * 512 + second * second_stride + first * first_stride, 32)
            blocks.append(a_ref[pl.ds(start, 32), :])
    return jnp.concatenate(blocks, axis=0)


def masked(b_ref, m_ref):
    parts = [
        b_ref[k * 128:(k + 1) * 128, :] * m_ref[k:k + 1, :].astype(jnp.bfloat16) for k in range(b_ref.shape[0] // 128)
    ]
    return jnp.concatenate(parts, axis=0)


def dot(left, right):
    return jnp.dot(left, right, preferred_element_type=jnp.float32)


def encode(value, step, out_ref, codes_ref):
    largest = jnp.maximum(jnp.max(jnp.abs(value), axis=1, keepdims=True), 1e-30)
    code = jnp.ceil(jnp.log2(largest) * STEPS)
    factor = jnp.exp2(code * (-1.0 / STEPS)) * LEVELS
    at = pl.ds(pl.multiple_of(step * TILE, TILE), TILE)
    out_ref[:, at] = jnp.round(value * factor).astype(jnp.int32).astype(jnp.int16)
    lane = lax.broadcasted_iota(jnp.int32, codes_ref.shape, 1)
    codes = jnp.where(lane == step, code, codes_ref[...])
    codes_ref[...] = codes
    width = out_ref.shape[1] - 128

    @pl.when(step == pl.num_programs(0) - 1)
    def _():
        out_ref[:, width:] = codes.astype(jnp.int32).astype(jnp.int16)


def decode(data_ref, code_ref, step):
    codes = code_ref[...].astype(jnp.int32).astype(jnp.float32)
    lane = lax.broadcasted_iota(jnp.int32, codes.shape, 1)
    code = jnp.sum(jnp.where(lane == step, codes, 0.0), axis=1, keepdims=True)
    factor = jnp.exp2(code * (1.0 / STEPS)) * (1.0 / LEVELS)
    return data_ref[...].astype(jnp.int32).astype(jnp.float32) * factor


def opposite_kernel(pos, a, b0, b1, m0, m1, p0, q0, p1, q1, *codes):
    step = pl.program_id(0)

    for kind, b, m, p, q in ((0, b0, m0, p0, q0), (1, b1, m1, p1, q1)):
        rows = left_rows(a, kind, (pos[1 + kind] + 2) % 4)
        sums = dot(rows, masked(b, m))
        encode(sums[:128], step, p, codes[2 * kind])
        encode(sums[128:], step, q, codes[2 * kind + 1])


def neighbour_kernel(pos, a, b0, b1, m0, m1, *refs):
    step = pl.program_id(0)
    taken, outs, codes = refs[:8], refs[8:12], refs[12:]
    for kind, b, m in ((0, b0, m0), (1, b1, m1)):
        right = masked(b, m)
        for way in range(2):
            first = (pos[1 + kind] + (1 if way == 0 else 3)) % 4
            sums = dot(left_rows(a, kind, first), right)
            got = decode(taken[4 * kind + 2 * way], taken[4 * kind + 2 * way + 1], step)
            if way == 0:
                sums = jnp.concatenate([sums[:128] + got, sums[128:]], axis=0)
            else:
                sums = jnp.concatenate([sums[:128], sums[128:] + got], axis=0)
            encode(sums, step, outs[2 * kind + way], codes[2 * kind + way])


def own_kernel(pos, a, b0, b1, m0, m1, *refs):
    step = pl.program_id(0)
    taken, outs, codes = refs[:8], refs[8:14], refs[14:]
    for kind, b, m in ((0, b0, m0), (1, b1, m1)):
        sums = dot(left_rows(a, kind, pos[1 + kind]), masked(b, m))
        for way in range(2):
            sums = sums + decode(taken[4 * kind + 2 * way], taken[4 * kind + 2 * way + 1], step)
        p, q, kept = outs[3 * kind:3 * kind + 3]
        kept[...] = sums
        second = (pos[2 - kind] + 2) % 4
        for z, out in ((0, p), (1, q)):
            encode(kept[pl.ds(pl.multiple_of(z * 128 + second * 32, 32), 32), :], step, out, codes[2 * kind + z])


def second_neighbour_kernel(pos, *refs):
    step = pl.program_id(0)
    taken, outs, codes = refs[:10], refs[10:14], refs[14:]
    for kind in range(2):
        kept = taken[5 * kind]
        for way in range(2):
            second = (pos[2 - kind] + (1 if way == 0 else 3)) % 4
            got = decode(taken[5 * kind + 1 + 2 * way], taken[5 * kind + 2 + 2 * way], step)
            parts = [kept[pl.ds(pl.multiple_of(z * 128 + second * 32, 32), 32), :] for z in range(2)]
            parts[way] = parts[way] + got
            encode(jnp.concatenate(parts, axis=0), step, outs[2 * kind + way], codes[2 * kind + way])


def second_own_kernel(pos, *refs):
    step = pl.program_id(0)
    taken, outs, codes, scratch = refs[:10], refs[10:14], refs[14:16], refs[16]
    for kind in range(2):
        kept = taken[5 * kind]
        second = pos[2 - kind]
        parts = [kept[pl.ds(pl.multiple_of(z * 128 + second * 32, 32), 32), :] for z in range(2)]
        sums = jnp.concatenate(parts, axis=0)
        for way in range(2):
            sums = sums + decode(taken[5 * kind + 1 + 2 * way], taken[5 * kind + 2 + 2 * way], step)
        scratch[...] = sums
        z = pos[0]
        encode(scratch[pl.ds(pl.multiple_of((1 - z) * 32, 32), 32), :], step, outs[2 * kind], codes[kind])
        outs[2 * kind + 1][...] = scratch[pl.ds(pl.multiple_of(z * 32, 32), 32), :]


def last_kernel(*refs):
    step = pl.program_id(0)
    taken, outs = refs[:6], refs[6:]
    for kind in range(2):
        sums = taken[3 * kind][...] + decode(taken[3 * kind + 1], taken[3 * kind + 2], step)
        outs[kind][...] = sums.astype(jnp.bfloat16)


def whole(shape):
    return pl.BlockSpec(shape, lambda j: (0, 0))


def pieces(rows, start=0):
    return pl.BlockSpec((rows, TILE), lambda j: (0, j + start))


def coded(rows, width):
    return [pieces(rows), pl.BlockSpec((rows, 128), lambda j: (0, width // 128))]


def twice(values):
    return [v for value in values for v in (value, value)]


def call(kernel, args, in_specs, outs, out_specs, scratch, width, name):
    return pl.pallas_call(
        kernel,
        grid=(width // TILE,),
        in_specs=in_specs,
        out_specs=out_specs,
        out_shape=outs,
        scratch_shapes=scratch,
        compiler_params=pltpu.CompilerParams(vmem_limit_bytes=VMEM_LIMIT),
        cost_estimate=pl.CostEstimate(flops=1000000, bytes_accessed=1000000, transcendentals=0),
        name=name,
    )(*args)


SMEM = pl.BlockSpec(memory_space=pltpu.SMEM)


def per_device(amplitudes, amplitude_mask, integrals, integral_mask, tile_order):
    pair_count, full_width = amplitudes.shape
    tile_count = amplitude_mask.shape[1]
    depth, columns = integrals.shape
    width = columns // (2 * N_CHUNK)
    tiles = width // TILE
    row = lax.axis_index("row")
    pos = jnp.stack([row // 16, (row // 4) % 4, row % 4]).astype(jnp.int32)
    shaped = (
        amplitudes.reshape(pair_count, tile_count, full_width // tile_count)
        * amplitude_mask.astype(jnp.bfloat16)[:, :, None]
    )
    ordered = jnp.take(shaped, tile_order, axis=1).reshape(pair_count, full_width)
    placed = lax.all_to_all(ordered, "row", split_axis=1, concat_axis=0, tiled=True)
    col = lax.axis_index("col")
    beside = lax.ppermute(placed, "col", [(0, 1), (1, 0), (2, 3), (3, 2)])
    over = lax.ppermute(placed, "col", [(0, 2), (1, 3), (2, 0), (3, 1)])
    both = lax.ppermute(over, "col", [(0, 1), (1, 0), (2, 3), (3, 2)])
    core, z_hi = col % 2, col // 2
    even, odd = jnp.where(core == 0, placed, beside), jnp.where(core == 0, beside, placed)
    far_even, far_odd = jnp.where(core == 0, over, both), jnp.where(core == 0, both, over)
    four = [
        jnp.where(z_hi == 0, even, far_even),
        jnp.where(z_hi == 0, odd, far_odd),
        jnp.where(z_hi == 0, far_even, even),
        jnp.where(z_hi == 0, far_odd, odd),
    ]
    left = jnp.stack([v.reshape(32, 8, depth) for v in four], axis=1).reshape(1024, depth)
    flags = jnp.repeat(integral_mask.astype(jnp.float32), 128, axis=1)

    def sent(rows):
        return jax.ShapeDtypeStruct((rows, width + 128), jnp.int16)

    def codes(rows, count):
        return [pltpu.VMEM((rows, 128), jnp.float32)] * count

    finals = []
    stage = []

    def product_args(j):
        args = [pos, left, integrals, integrals, flags, flags]
        starts = [2 * j * tiles, (2 * j + 1) * tiles]
        specs = [SMEM, whole((1024, depth))]
        specs += [pieces(depth, s) for s in starts] + [pieces(integral_mask.shape[0], s) for s in starts]
        return args, specs

    def begin(j):
        args, specs = product_args(j)
        p0, q0, p1, q1 = call(
            opposite_kernel, args, specs, [sent(128)] * 4, [whole((128, width + 128))] * 4, codes(128, 4), width,
            "opposite",
        )
        return [send(p0, FORWARD[0]), send(q0, BACKWARD[0]), send(p1, FORWARD[1]), send(q1, BACKWARD[1])]

    def second(j, got):
        args, specs = product_args(j)
        outs = call(
            neighbour_kernel, args + twice(got), specs + coded(128, width) * 4, [sent(256)] * 4,
            [whole((256, width + 128))] * 4, codes(256, 4), width, "neighbour",
        )
        return [send(outs[2 * k + w], (FORWARD, BACKWARD)[w][k]) for k in range(2) for w in range(2)]

    def third(j, got):
        args, specs = product_args(j)
        kept = jax.ShapeDtypeStruct((256, width), jnp.float32)
        p0, q0, k0, p1, q1, k1 = call(
            own_kernel, args + twice(got), specs + coded(256, width) * 4, [sent(32), sent(32), kept] * 2,
            [whole((32, width + 128))] * 2 + [pieces(256)] + [whole((32, width + 128))] * 2 + [pieces(256)],
            codes(32, 4), width, "own",
        )
        return [k0, k1], [send(p0, FORWARD[1]), send(q0, BACKWARD[1]), send(p1, FORWARD[0]), send(q1, BACKWARD[0])]

    def fourth(kept, got):
        args = [pos, kept[0]] + twice(got[:2]) + [kept[1]] + twice(got[2:])
        specs = [SMEM] + ([pieces(256)] + coded(32, width) * 2) * 2
        outs = call(
            second_neighbour_kernel, args, specs, [sent(64)] * 4, [whole((64, width + 128))] * 4, codes(64, 4), width,
            "second_neighbour",
        )
        return [send(outs[2 * k + w], (FORWARD, BACKWARD)[w][1 - k]) for k in range(2) for w in range(2)]

    def fifth(kept, got):
        args = [pos, kept[0]] + twice(got[:2]) + [kept[1]] + twice(got[2:])
        specs = [SMEM] + ([pieces(256)] + coded(64, width) * 2) * 2
        rest = jax.ShapeDtypeStruct((32, width), jnp.float32)
        p0, k0, p1, k1 = call(
            second_own_kernel, args, specs, [sent(32), rest] * 2, [whole((32, width + 128)), pieces(32)] * 2,
            codes(32, 2) + [pltpu.VMEM((64, TILE), jnp.float32)], width, "second_own",
        )
        return [k0, k1], [send(p0, ACROSS), send(p1, ACROSS)]

    def sixth(kept, got):
        args = [kept[0], got[0], got[0], kept[1], got[1], got[1]]
        specs = ([pieces(32)] + coded(32, width)) * 2
        return call(
            last_kernel, args, specs, [jax.ShapeDtypeStruct((32, width), jnp.bfloat16)] * 2, [pieces(32)] * 2, [],
            width, "last",
        )

    ones = [begin(j) for j in range(N_CHUNK)]
    twos = [second(j, ones[j]) for j in range(N_CHUNK)]
    for j in range(N_CHUNK):
        kept, got = third(j, twos[j])
        got = fourth(kept, got)
        rest, got = fifth(kept, got)
        finals += sixth(rest, got)
    summed = jnp.concatenate(finals, axis=1)
    return lax.all_to_all(summed, "col", split_axis=0, concat_axis=1, tiled=True)


def solution(mesh):
    in_specs = (
        P(("row", "col"), None),
        P(("row", "col"), None),
        P("row", "col"),
        P("row", "col"),
        P(),
    )
    out_specs = P(("row", "col"), None)
    return jax.shard_map(
        per_device, mesh=mesh, in_specs=in_specs, out_specs=out_specs, check_vma=False
    )
```

```python
import functools

import jax
import jax.numpy as jnp
from jax import lax
from jax.experimental import pallas as pl
from jax.experimental.pallas import tpu as pltpu
from jax.sharding import PartitionSpec as P

LEVELS = 32600.0
STEPS = 32.0
ROUNDER = 12582912.0
CODE_ROWS = 16
VMEM_LIMIT = 48 * 1024 * 1024


def shift(dz, dx, dy):
    pairs = []
    for index in range(32):
        z, x, y = index // 16, (index // 4) % 4, index % 4
        pairs.append((index, ((z + dz) % 2) * 16 + ((x + dx) % 4) * 4 + (y + dy) % 4))
    return pairs


FORWARD = (shift(0, 1, 0), shift(0, 0, 1))
BACKWARD = (shift(0, -1, 0), shift(0, 0, -1))
ACROSS = shift(1, 0, 0)


def send(value, pairs):
    return lax.ppermute(value, "row", pairs)


def send_col(value, step):
    return lax.ppermute(value, "col", [(c, c ^ step) for c in range(4)])


def encode(value, out_ref):
    rows, width = value.shape
    largest = jnp.max(jnp.max(jnp.abs(value.reshape(rows // 8, 8, width)), axis=0), axis=0, keepdims=True)
    code = jnp.ceil(jnp.log2(jnp.maximum(largest, 1e-30)) * STEPS)
    factor = jnp.exp2(code * (-1.0 / STEPS)) * LEVELS
    rounded = (value * factor + ROUNDER) - ROUNDER
    out_ref[:rows, :] = rounded.astype(jnp.int32).astype(jnp.int16)
    out_ref[rows:, :] = jnp.broadcast_to(code, (CODE_ROWS, width)).astype(jnp.int32).astype(jnp.int16)


def decode(in_ref):
    rows = in_ref.shape[0] - CODE_ROWS
    code = in_ref[rows:, :].astype(jnp.int32).astype(jnp.float32)[:1]
    factor = jnp.exp2(code * (1.0 / STEPS)) * (1.0 / LEVELS)
    return in_ref[:rows, :].astype(jnp.int32).astype(jnp.float32) * factor


def copy_rows(a_ref, left_ref, at, kind, first, z):
    first_stride, second_stride = (128, 32) if kind == 0 else (32, 128)
    for second in range(4):
        start = pl.multiple_of(z * 512 + second * second_stride + first * first_stride, 32)
        left_ref[at + second * 32:at + second * 32 + 32, :] = a_ref[pl.ds(start, 32), :]


def product(left_ref, b_ref, m_ref):
    parts = [b_ref[k * 128:(k + 1) * 128, :] * m_ref[k:k + 1, :] for k in range(b_ref.shape[0] // 128)]
    return jnp.dot(left_ref[...], jnp.concatenate(parts, axis=0), preferred_element_type=jnp.float32)


def arrange_kernel(order, values, flags, out, kept):
    tiles = flags.shape[1]
    for t in range(tiles):
        at = slice(t * 128, (t + 1) * 128)
        kept[:, at] = values[:, at] * flags[:, t:t + 1].astype(jnp.float32).astype(jnp.bfloat16)
    for k in range(tiles):
        out[:, k * 128:(k + 1) * 128] = kept[:, pl.ds(pl.multiple_of(order[k] * 128, 128), 128)]


def opposite_kernel(kind, pos, a, b, m, p, q, left):
    @pl.when(pl.program_id(0) == 0)
    def _():
        first = (pos[1 + kind] + 2) % 4
        copy_rows(a, left, 0, kind, first, 0)
        copy_rows(a, left, 128, kind, first, 1)

    sums = product(left, b, m)
    encode(sums[:128], p)
    encode(sums[128:], q)


def rest_kernel(kind, pos, a, b, m, ip, iq, later, own, left):
    @pl.when(pl.program_id(0) == 0)
    def _():
        here = pos[1 + kind]
        ahead, behind = (here + 1) % 4, (here + 3) % 4
        for at, (first, z) in enumerate(((ahead, 0), (behind, 1), (ahead, 1), (behind, 0), (here, 0), (here, 1))):
            copy_rows(a, left, at * 128, kind, first, z)

    sums = product(left, b, m)
    later[...] = sums[:256]
    encode(sums[256:384], ip)
    encode(sums[384:512], iq)
    own[...] = sums[512:]


def pass_on_kernel(later, p, q, dp, dq):
    encode(later[:128, :] + decode(p), dp)
    encode(later[128:, :] + decode(q), dq)


def gather_kernel(kind, pos, own, dp, ip, dq, iq, p, q, kept):
    kept[:128, :] = own[:128, :] + decode(dp) + decode(iq)
    kept[128:, :] = own[128:, :] + decode(ip) + decode(dq)
    second = (pos[2 - kind] + 2) % 4
    for z, out in ((0, p), (1, q)):
        encode(kept[pl.ds(pl.multiple_of(z * 128 + second * 32, 32), 32), :], out)


def second_pass_kernel(kind, pos, kept, p, q, np, nq):
    for way, got, out in ((0, p, np), (1, q, nq)):
        second = (pos[2 - kind] + (1 if way == 0 else 3)) % 4
        parts = [kept[pl.ds(pl.multiple_of(z * 128 + second * 32, 32), 32), :] for z in range(2)]
        parts[way] = parts[way] + decode(got)
        encode(jnp.concatenate(parts, axis=0), out)


def second_gather_kernel(kind, pos, kept, p, q, out, rest, scratch):
    second = pos[2 - kind]
    parts = [kept[pl.ds(pl.multiple_of(z * 128 + second * 32, 32), 32), :] for z in range(2)]
    scratch[...] = jnp.concatenate(parts, axis=0) + decode(p) + decode(q)
    z = pos[0]
    encode(scratch[pl.ds(pl.multiple_of((1 - z) * 32, 32), 32), :], out)
    rest[...] = scratch[pl.ds(pl.multiple_of(z * 32, 32), 32), :]


def last_kernel(rest0, got0, rest1, got1, out0, out1):
    out0[...] = (rest0[...] + decode(got0)).astype(jnp.bfloat16)
    out1[...] = (rest1[...] + decode(got1)).astype(jnp.bfloat16)


SMEM = pl.BlockSpec(memory_space=pltpu.SMEM)


def call(kernel, args, ins, outs, tile, width, scratch=()):
    def spec(s):
        if isinstance(s, pl.BlockSpec):
            return s
        rows, start = s if isinstance(s, tuple) else (s, 0)
        return pl.BlockSpec((rows, tile), lambda j: (0, j + start))

    name = kernel.func.__name__ if isinstance(kernel, functools.partial) else kernel.__name__
    return pl.pallas_call(
        kernel,
        grid=(width // tile,),
        in_specs=[spec(s) for s in ins],
        out_specs=[spec(s.shape[0]) for s in outs],
        out_shape=outs,
        scratch_shapes=list(scratch),
        compiler_params=pltpu.CompilerParams(vmem_limit_bytes=VMEM_LIMIT),
        cost_estimate=pl.CostEstimate(flops=1000000, bytes_accessed=1000000, transcendentals=0),
        name=name,
    )(*args)


def per_device(amplitudes, amplitude_mask, integrals, integral_mask, tile_order):
    pair_count, full_width = amplitudes.shape
    depth, columns = integrals.shape
    width = columns // 2
    row, col = lax.axis_index("row"), lax.axis_index("col")
    pos = jnp.stack([row // 16, (row // 4) % 4, row % 4]).astype(jnp.int32)

    ordered = pl.pallas_call(
        arrange_kernel,
        in_specs=[SMEM, pl.BlockSpec(memory_space=pltpu.VMEM), pl.BlockSpec(memory_space=pltpu.VMEM)],
        out_specs=pl.BlockSpec(memory_space=pltpu.VMEM),
        out_shape=jax.ShapeDtypeStruct((pair_count, full_width), jnp.bfloat16),
        scratch_shapes=[pltpu.VMEM((pair_count, full_width), jnp.bfloat16)],
        name="arrange",
    )(tile_order, amplitudes, amplitude_mask)
    placed = lax.all_to_all(ordered, "row", split_axis=1, concat_axis=0, tiled=True)
    over = send_col(placed, 2)
    beside = send_col(placed, 1)
    both = send_col(over, 1)
    core, z_hi = col % 2, col // 2
    even, odd = jnp.where(core == 0, placed, beside), jnp.where(core == 0, beside, placed)
    far_even, far_odd = jnp.where(core == 0, over, both), jnp.where(core == 0, both, over)
    four = [
        jnp.where(z_hi == 0, even, far_even),
        jnp.where(z_hi == 0, odd, far_odd),
        jnp.where(z_hi == 0, far_even, even),
        jnp.where(z_hi == 0, far_odd, odd),
    ]
    left = jnp.stack([v.reshape(32, 8, depth) for v in four], axis=1).reshape(1024, depth)
    flags = jnp.repeat(integral_mask.astype(jnp.bfloat16), 128, axis=1)

    def sent(rows):
        return jax.ShapeDtypeStruct((rows + CODE_ROWS, width), jnp.int16)

    def floats(rows):
        return jax.ShapeDtypeStruct((rows, width), jnp.float32)

    coded = [128 + CODE_ROWS, 32 + CODE_ROWS, 64 + CODE_ROWS]
    whole_left = pl.BlockSpec((1024, depth), lambda j: (0, 0))
    flag_rows = integral_mask.shape[0]

    def left_scratch(rows):
        return [pltpu.VMEM((rows, depth), jnp.bfloat16)]

    def exchange(kind, p, q):
        return send(p, FORWARD[kind]), send(q, BACKWARD[kind])

    def operands(kind, tile):
        start = kind * (width // tile)
        return [pos, left, integrals, flags], [SMEM, whole_left, (depth, start), (flag_rows, start)]

    got, state = [None, None], [None, None]
    for kind in range(2):
        args, ins = operands(kind, 1792)
        p, q = call(
            functools.partial(opposite_kernel, kind), args, ins, [sent(128)] * 2, 1792, width, left_scratch(256)
        )
        got[kind] = exchange(kind, p, q)
    for kind in range(2):
        args, ins = operands(kind, 896)
        ip, iq, later, own = call(
            functools.partial(rest_kernel, kind), args, ins, [sent(128)] * 2 + [floats(256)] * 2, 896, width,
            left_scratch(768),
        )
        state[kind] = (exchange(kind, ip, iq), later, own)
    kept = [None, None]
    for kind in range(2):
        free, later, own = state[kind]
        dp, dq = call(pass_on_kernel, [later, *got[kind]], [256, coded[0], coded[0]], [sent(128)] * 2, 896, width)
        state[kind] = (free, exchange(kind, dp, dq), own)
    for kind in range(2):
        free, bound, own = state[kind]
        p, q, kept[kind] = call(
            functools.partial(gather_kernel, kind), [pos, own, bound[0], free[0], bound[1], free[1]],
            [SMEM, 256] + [coded[0]] * 4, [sent(32)] * 2 + [floats(256)], 896, width,
        )
        got[kind] = exchange(1 - kind, p, q)
    for kind in range(2):
        p, q = call(
            functools.partial(second_pass_kernel, kind), [pos, kept[kind], *got[kind]],
            [SMEM, 256, coded[1], coded[1]], [sent(64)] * 2, 1792, width,
        )
        got[kind] = exchange(1 - kind, p, q)
    rest = [None, None]
    for kind in range(2):
        p, rest[kind] = call(
            functools.partial(second_gather_kernel, kind), [pos, kept[kind], *got[kind]],
            [SMEM, 256, coded[2], coded[2]], [sent(32), floats(32)], 1792, width,
            [pltpu.VMEM((64, 1792), jnp.float32)],
        )
        got[kind] = send(p, ACROSS)
    halves = call(
        last_kernel, [rest[0], got[0], rest[1], got[1]], [32, coded[1], 32, coded[1]],
        [jax.ShapeDtypeStruct((32, width), jnp.bfloat16)] * 2, 1792, width,
    )
    summed = jnp.concatenate(halves, axis=1).reshape(4, 8, columns)
    pieces = [lax.dynamic_index_in_dim(summed, col, 0, keepdims=False)]
    for step in (1, 2, 3):
        pieces.append(send_col(lax.dynamic_index_in_dim(summed, col ^ step, 0, keepdims=False), step))
    pair = [jnp.where(core == 0, pieces[k], pieces[k ^ 1]) for k in range(4)]
    blocks = [jnp.where(z_hi == 0, pair[k], pair[k ^ 2]) for k in range(4)]
    return jnp.concatenate(blocks, axis=1)


def solution(mesh):
    in_specs = (
        P(("row", "col"), None),
        P(("row", "col"), None),
        P("row", "col"),
        P("row", "col"),
        P(),
    )
    out_specs = P(("row", "col"), None)
    return jax.shard_map(
        per_device, mesh=mesh, in_specs=in_specs, out_specs=out_specs, check_vma=False
    )
```

```python
import functools

import jax
import jax.numpy as jnp
from jax import lax
from jax.experimental import pallas as pl
from jax.experimental.pallas import tpu as pltpu
from jax.sharding import PartitionSpec as P

LEVELS = 32600.0
STEPS = 32.0
ROUNDER = 12582912.0
CODES = (32, 128)
VMEM_LIMIT = 24 * 1024 * 1024
TILE = 896


def shift(dz, dx, dy):
    pairs = []
    for index in range(32):
        z, x, y = index // 16, (index // 4) % 4, index % 4
        pairs.append((index, ((z + dz) % 2) * 16 + ((x + dx) % 4) * 4 + (y + dy) % 4))
    return pairs


FORWARD = (shift(0, 1, 0), shift(0, 0, 1))
BACKWARD = (shift(0, -1, 0), shift(0, 0, -1))
ACROSS = shift(1, 0, 0)
DIAGONAL = [(r * 4 + c, s * 4 + (c ^ 2)) for r, s in ACROSS for c in range(4)]


def send(value, pairs):
    return lax.ppermute(value, "row", pairs)


def send_col(value, step):
    return lax.ppermute(value, "col", [(c, c ^ step) for c in range(4)])


def quantised(value):
    rows, tile = value.shape
    largest = jnp.max(jnp.max(jnp.abs(value.reshape(rows // 8, 8, tile)), axis=0), axis=0, keepdims=True)
    code = jnp.ceil(jnp.log2(jnp.maximum(largest, 1e-30)) * STEPS)
    factor = jnp.exp2(code * (-1.0 / STEPS)) * LEVELS
    rounded = (value * factor + ROUNDER) - ROUNDER
    return rounded.astype(jnp.int32).astype(jnp.int16), code


def finish(out_ref, code_ref):
    rows, width = out_ref.shape[0], out_ref.shape[1] - 128
    out_ref[:32, width:] = code_ref[...].astype(jnp.int32).astype(jnp.int16)
    if rows > 32:
        out_ref[32:, width:] = jnp.zeros((rows - 32, 128), jnp.int16)


def encode(value, out_ref, code_ref):
    step, tile = pl.program_id(0), value.shape[1]
    out_ref[:, pl.ds(pl.multiple_of(step * tile, 128), tile)], code = quantised(value)

    @pl.when(step == 0)
    def _():
        code_ref[...] = jnp.zeros(CODES, jnp.float32)

    for i in range(tile // 128):
        code_ref[pl.ds(step * (tile // 128) + i, 1), :] = code[:, i * 128:(i + 1) * 128]

    @pl.when(step == pl.num_programs(0) - 1)
    def _():
        finish(out_ref, code_ref)


def encode_at(value, t, out_ref, code_ref):
    count = TILE // 128
    out_ref[:, columns_of(t)], code = quantised(value)
    for i in range(count):
        code_ref[pl.ds(t * count + i, 1), :] = code[:, i * 128:(i + 1) * 128]


def columns_of(t):
    return pl.ds(pl.multiple_of(t * TILE, 128), TILE)


def each_tile(width):
    return pl.loop(0, width // TILE)


def factors(code_ref, factor_ref, tile):
    step, count = pl.program_id(0), tile // 128

    @pl.when(step == 0)
    def _():
        factor_ref[...] = jnp.exp2(code_ref[...].astype(jnp.int32).astype(jnp.float32) * (1.0 / STEPS)) * (1.0 / LEVELS)

    return jnp.concatenate([factor_ref[pl.ds(step * count + i, 1), :] for i in range(count)], axis=1)


def wide(data_ref):
    return data_ref[...].astype(jnp.int32).astype(jnp.float32)


def decode(data_ref, code_ref, factor_ref):
    return wide(data_ref) * factors(code_ref, factor_ref, data_ref.shape[1])


def copy_rows(parts, left_ref, at, kind, first, z):
    first_stride, second_stride = (4, 1) if kind == 0 else (1, 4)
    for second in range(4):
        start = pl.multiple_of((z * 16 + second * second_stride + first * first_stride) * 16, 16)
        for part in parts:
            left_ref[at:at + 16, :] = part[pl.ds(start, 16), :]
            at += 16


def arrange_kernel(order, values, flags, out, kept):
    tiles = flags.shape[1]
    for t in range(tiles):
        at = slice(t * 128, (t + 1) * 128)
        kept[:, at] = values[:, at] * flags[:, t:t + 1].astype(jnp.float32).astype(jnp.bfloat16)
    for k in range(tiles):
        out[:, k * 128:(k + 1) * 128] = kept[:, pl.ds(pl.multiple_of(order[k] * 128, 128), 128)]


def clear(*code_refs):
    for code_ref in code_refs:
        code_ref[...] = jnp.zeros(CODES, jnp.float32)


def dot(left, right):
    return jnp.dot(left, right, preferred_element_type=jnp.float32)


def opposite_rows(pos, a, left):
    for kind in range(2):
        first = (pos[1 + kind] + 2) % 4
        copy_rows((a,), left.at[kind], 0, kind, first, 0)
        copy_rows((a,), left.at[kind], 64, kind, first, 1)


def begin_kernel(pos, a, b0, b1, m0, m1, p0, q0, p1, q1, w0, w1, left, *code_refs):
    @pl.when(pl.program_id(0) == 0)
    def _():
        opposite_rows(pos, a, left)

    for kind, b, m, p, q, w in ((0, b0, m0, p0, q0, w0), (1, b1, m1, p1, q1, w1)):
        for k in range(b.shape[0] // 128):
            w[k * 128:(k + 1) * 128, :] = b[k * 128:(k + 1) * 128, :] * m[k:k + 1, :]
        sums = dot(left[kind], w[...])
        encode(sums[:64], p, code_refs[2 * kind])
        encode(sums[64:], q, code_refs[2 * kind + 1])


def opposite_kernel(pos, w0, w1, a, p0, q0, p1, q1, left, *code_refs):
    clear(*code_refs)
    opposite_rows(pos, a, left)
    for kind, w, p, q in ((0, w0, p0, q0), (1, w1, p1, q1)):
        @each_tile(w.shape[1])
        def _(t):
            sums = dot(left[kind], w[:, columns_of(t)])
            encode_at(sums[:64], t, p, code_refs[2 * kind])
            encode_at(sums[64:], t, q, code_refs[2 * kind + 1])

        finish(p, code_refs[2 * kind])
        finish(q, code_refs[2 * kind + 1])


def free_kernel(pos, w0, w1, near, far, p0, q0, p1, q1, left, *code_refs):
    clear(*code_refs)
    for kind, w, p, q in ((0, w0, p0, q0), (1, w1, p1, q1)):
        copy_rows((near, far), left, 0, kind, (pos[1 + kind] + 1) % 4, 1)
        copy_rows((near, far), left, 128, kind, (pos[1 + kind] + 3) % 4, 0)

        @each_tile(w.shape[1])
        def _(t):
            sums = dot(left[...], w[:, columns_of(t)])
            encode_at(sums[:128], t, p, code_refs[2 * kind])
            encode_at(sums[128:], t, q, code_refs[2 * kind + 1])

        finish(p, code_refs[2 * kind])
        finish(q, code_refs[2 * kind + 1])


def own_kernel(pos, w0, w1, near, far, own0, own1, left):
    for kind, w, own in ((0, w0, own0), (1, w1, own1)):
        for z in range(2):
            copy_rows((near, far), left, z * 128, kind, pos[1 + kind], z)

        @each_tile(w.shape[1])
        def _(t):
            own[:, columns_of(t)] = dot(left[...], w[:, columns_of(t)])


def read_factors(ref, factor_ref):
    codes = ref[:32, ref.shape[1] - 128:].astype(jnp.int32).astype(jnp.float32)
    factor_ref[...] = jnp.exp2(codes * (1.0 / STEPS)) * (1.0 / LEVELS)


def decode_at(ref, factor_ref, t):
    count = TILE // 128
    scale = jnp.concatenate([factor_ref[pl.ds(t * count + i, 1), :] for i in range(count)], axis=1)
    return ref[:, columns_of(t)].astype(jnp.int32).astype(jnp.float32) * scale


def pass_on_kernel(pos, w0, w1, near, far, *refs):
    outs, left, factor_refs, code_refs = refs[8:12], refs[12], refs[13:21], refs[21:]
    clear(*code_refs)
    for kind, w in ((0, w0), (1, w1)):
        got, scale = refs[4 * kind:4 * kind + 4], factor_refs[4 * kind:4 * kind + 4]
        copy_rows((near, far), left, 0, kind, (pos[1 + kind] + 1) % 4, 0)
        copy_rows((near, far), left, 128, kind, (pos[1 + kind] + 3) % 4, 1)
        for ref, factor in zip(got, scale):
            read_factors(ref, factor)

        @each_tile(w.shape[1])
        def _(t):
            sums = dot(left[...], w[:, columns_of(t)])
            for way in range(2):
                n, f = (decode_at(got[2 * part + way], scale[2 * part + way], t) for part in range(2))
                mixed = []
                for second in range(4):
                    mixed += [n[second * 16:second * 16 + 16], f[second * 16:second * 16 + 16]]
                value = sums[way * 128:way * 128 + 128] + jnp.concatenate(mixed, axis=0)
                encode_at(value, t, outs[2 * kind + way], code_refs[2 * kind + way])

        for way in range(2):
            finish(outs[2 * kind + way], code_refs[2 * kind + way])


def stage_one(refs, code_refs, scratch):
    own0, own1, dp, iq, ip, dq = refs
    tile = own0.shape[1]
    fdp, fiq, fip, fdq = (factors(c, f, tile) for c, f in zip(code_refs, scratch))
    return [own0[...] + wide(dp) * fdp + wide(iq) * fiq, own1[...] + wide(ip) * fip + wide(dq) * fdq]


def second_opposite_kernel(pos, *refs):
    for kind in range(2):
        some, outs, scratch = refs[10 * kind:10 * kind + 10], refs[20 + 2 * kind:22 + 2 * kind], refs[24 + 6 * kind:]
        sums = stage_one(some[:6], some[6:10], scratch[:4])
        encode(sums[0], outs[0], scratch[4])
        encode(sums[1], outs[1], scratch[5])


def keep_kernel(pos, *refs):
    for kind in range(2):
        own, dp, dpc, iq, iqc, ip, ipc, dq, dqc = refs[9 * kind:9 * kind + 9]
        out, scratch = refs[18 + kind], refs[20 + 4 * kind:24 + 4 * kind]
        out[:128, :] = own[:128, :] + decode(dp, dpc, scratch[0]) + decode(iq, iqc, scratch[1])
        out[128:, :] = own[128:, :] + decode(ip, ipc, scratch[2]) + decode(dq, dqc, scratch[3])


def block(kept, z, second, t):
    return kept[pl.ds(pl.multiple_of(z * 128 + second * 32, 32), 32), columns_of(t)]


def second_neighbour_kernel(pos, *refs):
    outs, factor_refs, code_refs = refs[6:10], refs[10:14], refs[14:]
    clear(*code_refs)
    for kind in range(2):
        kept, got = refs[3 * kind], refs[3 * kind + 1:3 * kind + 3]
        for way in range(2):
            read_factors(got[way], factor_refs[2 * kind + way])

        @each_tile(kept.shape[1])
        def _(t):
            for way in range(2):
                second = (pos[2 - kind] + (1 if way == 0 else 3)) % 4
                parts = [block(kept, z, second, t) for z in range(2)]
                parts[way] = parts[way] + decode_at(got[way], factor_refs[2 * kind + way], t)
                encode_at(jnp.concatenate(parts, axis=0), t, outs[2 * kind + way], code_refs[2 * kind + way])

        for way in range(2):
            finish(outs[2 * kind + way], code_refs[2 * kind + way])


def spread_kernel(pos, *refs):
    outs, sums, factor_refs, code_refs = refs[6:10], refs[10], refs[11:15], refs[15:]
    clear(*code_refs)
    z = pos[0]
    for kind in range(2):
        for way in range(2):
            read_factors(refs[3 * kind + 1 + way], factor_refs[2 * kind + way])

    def rows(h, far):
        at = [pl.multiple_of(kind * 64 + h * 32 + far * 16, 16) for kind in range(2)]
        return jnp.concatenate([sums[pl.ds(a, 16), :] for a in at], axis=0)

    @each_tile(refs[0].shape[1])
    def _(t):
        for kind in range(2):
            kept, got = refs[3 * kind], refs[3 * kind + 1:3 * kind + 3]
            value = jnp.concatenate([block(kept, h, pos[2 - kind], t) for h in range(2)], axis=0)
            for way in range(2):
                value = value + decode_at(got[way], factor_refs[2 * kind + way], t)
            sums[kind * 64:kind * 64 + 64, :] = value
        for at, (h, far) in enumerate(((1 - z, 0), (z, 1), (1 - z, 1))):
            encode_at(rows(h, far), t, outs[at], code_refs[at])
        outs[3][:, columns_of(t)] = rows(z, 0)

    for at in range(3):
        finish(outs[at], code_refs[at])


def last_kernel(pos, rest, a, b, c, near0, near1, far0, far1, f0, f1, f2):
    for ref, factor in ((a, f0), (b, f1), (c, f2)):
        read_factors(ref, factor)

    @each_tile(rest.shape[1])
    def _(t):
        at = columns_of(t)
        near = (rest[:, at] + decode_at(a, f0, t)).astype(jnp.bfloat16)
        far = (decode_at(b, f1, t) + decode_at(c, f2, t)).astype(jnp.bfloat16)
        near0[:, at], near1[:, at] = near[:16], near[16:]
        far0[:, at], far1[:, at] = far[:16], far[16:]


COST = pl.CostEstimate(flops=1000, bytes_accessed=1000, transcendentals=0)


class Calls:
    def __init__(self, pos, width, first):
        self.pos, self.width, self.last = pos, width, first

    def in_vmem(self, kernel, values, outs, scratch=(), after=()):
        after = [self.last, *after]
        skipped = len(after)
        name = kernel.func.__name__ if isinstance(kernel, functools.partial) else kernel.__name__
        vmem = pl.BlockSpec(memory_space=pltpu.VMEM)
        results = pl.pallas_call(
            lambda *refs: kernel(refs[skipped], *refs[skipped + 1:]),
            in_specs=[pl.BlockSpec(memory_space=pl.ANY)] * skipped + [pl.BlockSpec(memory_space=pltpu.SMEM)]
            + [vmem] * len(values),
            out_specs=[vmem] * len(outs),
            out_shape=outs,
            scratch_shapes=list(scratch),
            compiler_params=pltpu.CompilerParams(vmem_limit_bytes=VMEM_LIMIT),
            cost_estimate=COST,
            name=name,
        )(*after, self.pos, *values)
        self.last = results[0]
        return results

    def columns(self, value, rows, start=0):
        return [(value, lambda tile: pl.BlockSpec((rows, tile), lambda j, pos: (0, j + start * self.width // tile)))]

    def whole(self, value):
        return [(value, lambda tile: pl.BlockSpec(value.shape, lambda j, pos: (0, 0)))]

    def codes(self, value):
        return [(value, lambda tile: pl.BlockSpec(CODES, lambda j, pos: (0, self.width // 128)))]

    def coded(self, value, rows):
        return self.columns(value, rows) + self.codes(value)

    def some_rows(self, value, which):
        return [(value, lambda tile: pl.BlockSpec((32, tile), lambda j, pos: (which(pos), j)))]

    def __call__(self, kernel, operands, outs, tile, scratch=(), after=()):
        after = [self.last, *after]
        out_specs = []
        for o in outs:
            if o.dtype == jnp.int16:
                out_specs.append(pl.BlockSpec(o.shape, lambda j, pos: (0, 0)))
            else:
                out_specs.append(pl.BlockSpec((o.shape[0], tile), lambda j, pos: (0, j)))
        skipped = len(after)
        name = kernel.func.__name__ if isinstance(kernel, functools.partial) else kernel.__name__
        results = pl.pallas_call(
            lambda pos, *refs: kernel(pos, *refs[skipped:]),
            grid_spec=pltpu.PrefetchScalarGridSpec(
                num_scalar_prefetch=1,
                grid=(self.width // tile,),
                in_specs=[pl.BlockSpec(memory_space=pl.ANY)] * skipped + [spec(tile) for _, spec in operands],
                out_specs=out_specs,
                scratch_shapes=list(scratch),
            ),
            out_shape=outs,
            compiler_params=pltpu.CompilerParams(vmem_limit_bytes=VMEM_LIMIT),
            cost_estimate=COST,
            name=name,
        )(self.pos, *after, *[value for value, _ in operands])
        self.last = results[0]
        return results


def scales(count):
    return [pltpu.VMEM(CODES, jnp.float32)] * count


def per_device(amplitudes, amplitude_mask, integrals, integral_mask, tile_order):
    pair_count, full_width = amplitudes.shape
    depth, columns = integrals.shape
    width = columns // 2
    row, col = lax.axis_index("row"), lax.axis_index("col")
    core, z_hi = col % 2, col // 2
    pos = jnp.stack([row // 16, (row // 4) % 4, row % 4]).astype(jnp.int32)
    flags = jnp.repeat(integral_mask.astype(jnp.bfloat16), 128, axis=1)

    ordered = pl.pallas_call(
        arrange_kernel,
        in_specs=[pl.BlockSpec(memory_space=pltpu.SMEM)] + [pl.BlockSpec(memory_space=pltpu.VMEM)] * 2,
        out_specs=pl.BlockSpec(memory_space=pltpu.VMEM),
        out_shape=jax.ShapeDtypeStruct((pair_count, full_width), jnp.bfloat16),
        scratch_shapes=[pltpu.VMEM((pair_count, full_width), jnp.bfloat16)],
        name="arrange",
    )(tile_order, amplitudes, amplitude_mask)
    placed = lax.all_to_all(ordered, "row", split_axis=1, concat_axis=0, tiled=True)

    def both_cores(mine, other):
        even, odd = jnp.where(core == 0, mine, other), jnp.where(core == 0, other, mine)
        return jnp.stack([even.reshape(32, 8, depth), odd.reshape(32, 8, depth)], axis=1).reshape(512, depth)

    over = send_col(placed, 2)
    near = both_cores(placed, send_col(placed, 1))

    def sent(rows):
        return jax.ShapeDtypeStruct((rows, width + 128), jnp.int16)

    def floats(rows):
        return jax.ShapeDtypeStruct((rows, width), jnp.float32)

    call = Calls(pos, width, placed)

    def kept(rows):
        return pltpu.VMEM((rows, width), jnp.float32)

    def left_rows(*rows):
        return [pltpu.VMEM((*rows, depth), jnp.bfloat16)]

    def exchange_both(outs, ahead=(), turned=0):
        if ahead:
            *outs, _ = lax.optimization_barrier((*outs, *ahead))[:5]
        return [send(outs[2 * k + w], (FORWARD, BACKWARD)[w][k ^ turned]) for k in range(2) for w in range(2)]

    flag_rows = integral_mask.shape[0]
    results = call(
        begin_kernel,
        call.whole(near) + call.columns(integrals, depth, 0) + call.columns(integrals, depth, 1)
        + call.columns(flags, flag_rows, 0) + call.columns(flags, flag_rows, 1),
        [sent(64)] * 4 + [pltpu.VMEM((depth, width), jnp.bfloat16)] * 2, TILE, left_rows(2, 128) + scales(4),
    )
    n, weights = exchange_both(results[:4]), list(results[4:])
    over, _ = lax.optimization_barrier((over, call.last))
    far = both_cores(over, send_col(over, 1))
    f = exchange_both(call.in_vmem(opposite_kernel, weights + [far], [sent(64)] * 4, left_rows(2, 128) + scales(4)), n)
    i = exchange_both(
        call.in_vmem(free_kernel, weights + [near, far], [sent(128)] * 4, left_rows(256) + scales(4), n), f
    )
    operands = [v for k in range(2) for v in (*n[2 * k:2 * k + 2], *f[2 * k:2 * k + 2])]
    d = exchange_both(
        call.in_vmem(pass_on_kernel, weights + [near, far] + operands, [sent(128)] * 4, left_rows(256) + scales(12)), i
    )
    own = call.in_vmem(own_kernel, weights + [near, far], [kept(256)] * 2, left_rows(256), i)

    def arrived(kind):
        (ip, iq), (dp, dq) = i[2 * kind:2 * kind + 2], d[2 * kind:2 * kind + 2]
        return dp, iq, ip, dq

    operands = []
    for kind in range(2):
        def opposite(pos, kind=kind):
            return (pos[2 - kind] + 2) % 4

        for z in range(2):
            operands += call.some_rows(own[kind], lambda pos, z=z, at=opposite: z * 4 + at(pos))
        for v in arrived(kind):
            operands += call.some_rows(v, opposite)
        for v in arrived(kind):
            operands += call.codes(v)
    got = exchange_both(call(second_opposite_kernel, operands, [sent(32)] * 4, 1792, scales(12)), turned=1)
    operands = []
    for kind in range(2):
        operands += call.columns(own[kind], 256) + [o for v in arrived(kind) for o in call.coded(v, 128)]
    sums = call(keep_kernel, operands, [kept(256)] * 2, 896, scales(8))
    got = exchange_both(
        call.in_vmem(second_neighbour_kernel, [sums[0], *got[:2], sums[1], *got[2:]], [sent(64)] * 4, scales(8)),
        turned=1,
    )
    a, b, c, rest = call.in_vmem(
        spread_kernel, [sums[0], *got[:2], sums[1], *got[2:]], [sent(32)] * 3 + [floats(32)],
        [pltpu.VMEM((128, TILE), jnp.float32)] + scales(7),
    )
    a, b, c = send(a, ACROSS), send_col(b, 2), lax.ppermute(c, ("row", "col"), DIAGONAL)
    outs = call.in_vmem(
        last_kernel, [rest, a, b, c], [jax.ShapeDtypeStruct((16, width), jnp.bfloat16)] * 4, scales(3)
    )
    summed = jnp.concatenate(outs, axis=1).reshape(2, 8, 2 * columns)
    mine = lax.dynamic_index_in_dim(summed, core, 0, keepdims=False)
    other = send_col(lax.dynamic_index_in_dim(summed, 1 - core, 0, keepdims=False), 1)
    even, odd = jnp.where(core == 0, mine, other), jnp.where(core == 0, other, mine)
    near_pair = [even[:, :columns], odd[:, :columns]]
    far_pair = [even[:, columns:], odd[:, columns:]]
    first = [jnp.where(z_hi == 0, u, v) for u, v in zip(near_pair, far_pair)]
    last = [jnp.where(z_hi == 0, v, u) for u, v in zip(near_pair, far_pair)]
    return jnp.concatenate(first + last, axis=1)


def solution(mesh):
    in_specs = (
        P(("row", "col"), None),
        P(("row", "col"), None),
        P("row", "col"),
        P("row", "col"),
        P(),
    )
    out_specs = P(("row", "col"), None)
    return jax.shard_map(
        per_device, mesh=mesh, in_specs=in_specs, out_specs=out_specs, check_vma=False
    )
```

```python
import functools

import jax
import jax.numpy as jnp
from jax import lax
from jax.experimental import pallas as pl
from jax.experimental.pallas import tpu as pltpu
from jax.sharding import PartitionSpec as P

LEVELS = 32600.0
STEPS = 32.0
ROUNDER = 12582912.0
CODES = (32, 128)
VMEM_LIMIT = 12 * 1024 * 1024
BEGIN_LIMIT = 36 * 1024 * 1024
TILE = 896


def shift(dz, dx, dy):
    pairs = []
    for index in range(32):
        z, x, y = index // 16, (index // 4) % 4, index % 4
        pairs.append((index, ((z + dz) % 2) * 16 + ((x + dx) % 4) * 4 + (y + dy) % 4))
    return pairs


FORWARD = (shift(0, 1, 0), shift(0, 0, 1))
BACKWARD = (shift(0, -1, 0), shift(0, 0, -1))
ACROSS = shift(1, 0, 0)
DIAGONAL = [(r * 4 + c, s * 4 + (c ^ 2)) for r, s in ACROSS for c in range(4)]


def send(value, pairs):
    return lax.ppermute(value, "row", pairs)


def send_col(value, step):
    return lax.ppermute(value, "col", [(c, c ^ step) for c in range(4)])


def quantised(value):
    rows, tile = value.shape
    largest = jnp.max(jnp.max(jnp.abs(value.reshape(rows // 8, 8, tile)), axis=0), axis=0, keepdims=True)
    code = jnp.ceil(jnp.log2(jnp.maximum(largest, 1e-30)) * STEPS)
    factor = jnp.exp2(code * (-1.0 / STEPS)) * LEVELS
    rounded = (value * factor + ROUNDER) - ROUNDER
    return rounded.astype(jnp.int32).astype(jnp.int16), code


def finish(out_ref, code_ref):
    rows = out_ref.shape[0]
    codes = code_ref[...].astype(jnp.int32).astype(jnp.int16)
    if rows == 16:
        width = out_ref.shape[1] - 256
        out_ref[:, width:width + 128] = codes[:16]
        out_ref[:, width + 128:] = codes[16:]
        return
    width = out_ref.shape[1] - 128
    out_ref[:32, width:] = codes
    if rows > 32:
        out_ref[32:, width:] = jnp.zeros((rows - 32, 128), jnp.int16)


def encode(value, t, out_ref, code_ref):
    count = TILE // 128
    out_ref[:, columns_of(t)], code = quantised(value)
    for i in range(count):
        code_ref[pl.ds(t * count + i, 1), :] = code[:, i * 128:(i + 1) * 128]


def columns_of(t):
    return pl.ds(pl.multiple_of(t * TILE, 128), TILE)


def each_tile(width, unroll=1):
    return pl.loop(0, width // TILE, unroll=unroll)


def copy_rows(parts, left_ref, at, kind, first, z):
    first_stride, second_stride = (4, 1) if kind == 0 else (1, 4)
    for second in range(4):
        start = pl.multiple_of((z * 16 + second * second_stride + first * first_stride) * 16, 16)
        for part in parts:
            left_ref[at:at + 16, :] = part[pl.ds(start, 16), :]
            at += 16


def arrange_kernel(order, values, flags, tile_flags, out, flags_out, kept):
    for l in range(tile_flags.shape[1]):
        wide = jnp.broadcast_to(tile_flags[:, l:l + 1].astype(jnp.float32), (tile_flags.shape[0], 128))
        flags_out[:, l * 128:(l + 1) * 128] = wide.astype(jnp.bfloat16)
    tiles = flags.shape[1]
    for t in range(tiles):
        at = slice(t * 128, (t + 1) * 128)
        kept[:, at] = values[:, at] * flags[:, t:t + 1].astype(jnp.float32).astype(jnp.bfloat16)
    for k in range(tiles):
        out[:, k * 128:(k + 1) * 128] = kept[:, pl.ds(pl.multiple_of(order[k] * 128, 128), 128)]


def clear(*code_refs):
    for code_ref in code_refs:
        code_ref[...] = jnp.zeros(CODES, jnp.float32)


def dot(left, right):
    return jnp.dot(left, right, preferred_element_type=jnp.float32)


def opposite_rows(pos, kind, a, left, at_p, at_q):
    first = (pos[1 + kind] + 2) % 4
    copy_rows((a,), left, at_p, kind, first, 0)
    copy_rows((a,), left, at_q, kind, first, 1)


def free_rows(pos, kind, a, left, at_p, at_q):
    copy_rows((a,), left, at_p, kind, (pos[1 + kind] + 1) % 4, 1)
    copy_rows((a,), left, at_q, kind, (pos[1 + kind] + 3) % 4, 0)


def begin_kernel(pos, b, m, a, p0, q0, p1, q1, w0, w1, left, sems, *code_refs):
    tiles = w0.shape[1] // TILE

    def copy(kind, t):
        w = (w0, w1)[kind]
        at = pl.ds(kind * tiles * TILE + t * TILE, TILE)
        return pltpu.make_async_copy(b.at[:, at], w.at[:, pl.ds(t * TILE, TILE)], sems.at[kind * tiles + t])

    for t in range(tiles):
        for kind in range(2):
            copy(kind, t).start()
    clear(*code_refs)
    for kind in range(2):
        opposite_rows(pos, kind, a, left.at[kind], 0, 128)
        free_rows(pos, kind, a, left.at[kind], 64, 192)
    for t in range(tiles):
        for kind, w, p, q in ((0, w0, p0, q0), (1, w1, p1, q1)):
            copy(kind, t).wait()
            at = slice(t * TILE, (t + 1) * TILE)
            flags = m[:, (kind * tiles + t) * TILE:(kind * tiles + t + 1) * TILE]
            for k in range(w.shape[0] // 128):
                rows = slice(k * 128, (k + 1) * 128)
                w[rows, at] = w[rows, at] * flags[k:k + 1, :]
            sums = dot(left[kind], w[:, at])
            encode(sums[:128], t, p, code_refs[2 * kind])
            encode(sums[128:], t, q, code_refs[2 * kind + 1])
    for ref, code_ref in zip((p0, q0, p1, q1), code_refs):
        finish(ref, code_ref)


def far_kernel(rows, pos, w0, w1, a, p0, q0, p1, q1, left, *code_refs):
    clear(*code_refs)
    for kind, w, p, q in ((0, w0, p0, q0), (1, w1, p1, q1)):
        rows(pos, kind, a, left, 0, 64)

        @each_tile(w.shape[1], 2)
        def _(t):
            sums = dot(left[...], w[:, columns_of(t)])
            encode(sums[:64], t, p, code_refs[2 * kind])
            encode(sums[64:], t, q, code_refs[2 * kind + 1])

        finish(p, code_refs[2 * kind])
        finish(q, code_refs[2 * kind + 1])


def own_kernel(pos, w0, w1, near, far, own0, own1, left):
    for kind, w, own in ((0, w0, own0), (1, w1, own1)):
        for z in range(2):
            copy_rows((near, far), left, z * 128, kind, pos[1 + kind], z)

        @each_tile(w.shape[1], 2)
        def _(t):
            own[:, columns_of(t)] = dot(left[...], w[:, columns_of(t)])


def read_factors(ref, factor_ref):
    if ref.shape[0] == 16:
        width = ref.shape[1] - 256
        codes = jnp.concatenate([ref[:, width:width + 128], ref[:, width + 128:]], axis=0)
    else:
        codes = ref[:32, ref.shape[1] - 128:]
    factor_ref[...] = jnp.exp2(codes.astype(jnp.int32).astype(jnp.float32) * (1.0 / STEPS)) * (1.0 / LEVELS)


def decode(ref, factor_ref, t, rows=slice(None)):
    count = TILE // 128
    scale = jnp.concatenate([factor_ref[pl.ds(t * count + i, 1), :] for i in range(count)], axis=1)
    return ref[rows, columns_of(t)].astype(jnp.int32).astype(jnp.float32) * scale


def pass_on_kernel(pos, w0, w1, near, far, *refs):
    outs, left, factor_refs, code_refs = refs[8:12], refs[12], refs[13:21], refs[21:]
    clear(*code_refs)
    for kind, w in ((0, w0), (1, w1)):
        got, scale = refs[4 * kind:4 * kind + 4], factor_refs[4 * kind:4 * kind + 4]
        copy_rows((near, far), left, 0, kind, (pos[1 + kind] + 1) % 4, 0)
        copy_rows((near, far), left, 128, kind, (pos[1 + kind] + 3) % 4, 1)
        for ref, factor in zip(got, scale):
            read_factors(ref, factor)

        @each_tile(w.shape[1], 2)
        def _(t):
            sums = dot(left[...], w[:, columns_of(t)])
            for way in range(2):
                n, f = (decode(got[2 * part + way], scale[2 * part + way], t, slice(0, 64)) for part in range(2))
                mixed = []
                for second in range(4):
                    mixed += [n[second * 16:second * 16 + 16], f[second * 16:second * 16 + 16]]
                value = sums[way * 128:way * 128 + 128] + jnp.concatenate(mixed, axis=0)
                encode(value, t, outs[2 * kind + way], code_refs[2 * kind + way])

        for way in range(2):
            finish(outs[2 * kind + way], code_refs[2 * kind + way])


def stage_one(refs, factor_refs, second, t):
    own, dp, dq, np, nq, ip, iq = refs
    fdp, fdq, fnp, fnq, fip, fiq = factor_refs
    here, above = (pl.ds(pl.multiple_of(z * 128 + second * 32, 32), 32) for z in range(2))
    near, far = (pl.ds(pl.multiple_of(start + second * 16, 16), 16) for start in (64, 0))

    def free(n, fn, f, ff):
        return jnp.concatenate([decode(n, fn, t, near), decode(f, ff, t, far)], axis=0)

    return [
        own[here, columns_of(t)] + decode(dp, fdp, t, here) + free(nq, fnq, iq, fiq),
        own[above, columns_of(t)] + decode(dq, fdq, t, here) + free(np, fnp, ip, fip),
    ]


def second_opposite_kernel(kind, pos, *refs):
    some, outs, factor_refs, code_refs = refs[:7], refs[7:9], refs[9:15], refs[15:]
    clear(*code_refs)
    for ref, factor in zip(some[1:], factor_refs):
        read_factors(ref, factor)

    @each_tile(some[0].shape[1], 2)
    def _(t):
        sums = stage_one(some, factor_refs, (pos[2 - kind] + 2) % 4, t)
        for z in range(2):
            encode(sums[z], t, outs[z], code_refs[z])

    for z in range(2):
        finish(outs[z], code_refs[z])


def second_neighbour_kernel(kind, pos, *refs):
    some, got, outs, factor_refs, code_refs = refs[:7], refs[7:9], refs[9:11], refs[11:19], refs[19:]
    clear(*code_refs)
    for ref, factor in zip(refs[1:9], factor_refs):
        read_factors(ref, factor)

    @each_tile(some[0].shape[1], 2)
    def _(t):
        for way in range(2):
            sums = stage_one(some, factor_refs[:6], (pos[2 - kind] + (1 if way == 0 else 3)) % 4, t)
            sums[way] = sums[way] + decode(got[way], factor_refs[6 + way], t)
            encode(jnp.concatenate(sums, axis=0), t, outs[way], code_refs[way])

    for way in range(2):
        finish(outs[way], code_refs[way])


def spread_kernel(kind, pos, *refs):
    some, got, outs, sums, factor_refs, code_refs = refs[:7], refs[7:9], refs[9:13], refs[13], refs[14:22], refs[22:]
    clear(*code_refs)
    z = pos[0]
    for ref, factor in zip(refs[1:9], factor_refs):
        read_factors(ref, factor)

    def rows(h, far):
        return sums[pl.ds(pl.multiple_of(h * 32 + far * 16, 16), 16), :]

    @each_tile(some[0].shape[1], 2)
    def _(t):
        value = jnp.concatenate(stage_one(some, factor_refs[:6], pos[2 - kind], t), axis=0)
        sums[...] = value + decode(got[0], factor_refs[6], t) + decode(got[1], factor_refs[7], t)
        for at, (h, far) in enumerate(((1 - z, 0), (z, 1), (1 - z, 1))):
            encode(rows(h, far), t, outs[at], code_refs[at])
        outs[3][:, columns_of(t)] = rows(z, 0)

    for at in range(3):
        finish(outs[at], code_refs[at])


def last_kernel(pos, rest, a, b, c, near, far, f0, f1, f2):
    for ref, factor in ((a, f0), (b, f1), (c, f2)):
        read_factors(ref, factor)

    @each_tile(rest.shape[1], 2)
    def _(t):
        at = columns_of(t)
        near[:, at] = (rest[:, at] + decode(a, f0, t)).astype(jnp.bfloat16)
        far[:, at] = (decode(b, f1, t) + decode(c, f2, t)).astype(jnp.bfloat16)


COST = pl.CostEstimate(flops=1000, bytes_accessed=1000, transcendentals=0)


class Calls:
    def __init__(self, pos, first):
        self.pos, self.last = pos, first

    def __call__(self, kernel, values, outs, scratch=(), after=(), in_hbm=(), limit=VMEM_LIMIT):
        after = [self.last, *after]
        skipped = len(after)
        name = kernel.func.__name__ if isinstance(kernel, functools.partial) else kernel.__name__
        vmem = pl.BlockSpec(memory_space=pltpu.VMEM)
        results = pl.pallas_call(
            lambda *refs: kernel(refs[skipped], *refs[skipped + 1:]),
            in_specs=[pl.BlockSpec(memory_space=pl.ANY)] * skipped
            + [pl.BlockSpec(memory_space=pltpu.SMEM)]
            + [pl.BlockSpec(memory_space=pltpu.HBM)] * len(in_hbm) + [vmem] * len(values),
            out_specs=[vmem] * len(outs),
            out_shape=outs,
            scratch_shapes=list(scratch),
            compiler_params=pltpu.CompilerParams(vmem_limit_bytes=limit),
            cost_estimate=COST,
            name=name,
        )(*after, self.pos, *in_hbm, *values)
        self.last = results[0]
        return results


def scales(count):
    return [pltpu.VMEM(CODES, jnp.float32)] * count


def per_device(amplitudes, amplitude_mask, integrals, integral_mask, tile_order):
    pair_count, full_width = amplitudes.shape
    depth, columns = integrals.shape
    width = columns // 2
    row, col = lax.axis_index("row"), lax.axis_index("col")
    core, z_hi = col % 2, col // 2
    pos = jnp.stack([row // 16, (row // 4) % 4, row % 4]).astype(jnp.int32)

    ordered, flags = pl.pallas_call(
        arrange_kernel,
        in_specs=[pl.BlockSpec(memory_space=pltpu.SMEM)] + [pl.BlockSpec(memory_space=pltpu.VMEM)] * 3,
        out_specs=[pl.BlockSpec(memory_space=pltpu.VMEM)] * 2,
        out_shape=[
            jax.ShapeDtypeStruct((pair_count, full_width), jnp.bfloat16),
            pltpu.VMEM((integral_mask.shape[0], columns), jnp.bfloat16),
        ],
        scratch_shapes=[pltpu.VMEM((pair_count, full_width), jnp.bfloat16)],
        name="arrange",
    )(tile_order, amplitudes, amplitude_mask, integral_mask)
    ordered, pos = lax.optimization_barrier((ordered, pos))
    placed = lax.all_to_all(ordered, "row", split_axis=1, concat_axis=0, tiled=True)

    def both_cores(mine, other):
        even, odd = jnp.where(core == 0, mine, other), jnp.where(core == 0, other, mine)
        return jnp.stack([even.reshape(32, 8, depth), odd.reshape(32, 8, depth)], axis=1).reshape(512, depth)

    over = send_col(placed, 2)
    near = both_cores(placed, send_col(placed, 1))

    def sent(rows):
        return jax.ShapeDtypeStruct((rows, width + max(128, 4096 // rows)), jnp.int16)

    def floats(rows):
        return jax.ShapeDtypeStruct((rows, width), jnp.float32)

    call = Calls(pos, placed)

    def kept(rows):
        return pltpu.VMEM((rows, width), jnp.float32)

    def left_rows(*rows):
        return [pltpu.VMEM((*rows, depth), jnp.bfloat16)]

    def exchange_both(outs, ahead=()):
        sends = []
        for k in range(2):
            p, q = outs[2 * k:2 * k + 2]
            if ahead:
                p, q, *_ = lax.optimization_barrier((p, q, *ahead[2 * k:2 * k + 2]))
            sends += [send(p, FORWARD[k]), send(q, BACKWARD[k])]
        return sends

    results = call(
        begin_kernel, [flags, near], [sent(128)] * 4 + [pltpu.VMEM((depth, width), jnp.bfloat16)] * 2,
        left_rows(2, 256) + [pltpu.SemaphoreType.DMA((columns // TILE,))] + scales(4), in_hbm=[integrals],
        limit=BEGIN_LIMIT,
    )
    n, weights = exchange_both(results[:4]), list(results[4:])
    over, _ = lax.optimization_barrier((over, call.last))
    far = both_cores(over, send_col(over, 1))

    def far_part(rows, after):
        return call(
            functools.partial(far_kernel, rows), weights + [far], [sent(64)] * 4, left_rows(128) + scales(4), after
        )

    f = exchange_both(far_part(opposite_rows, ()), n)
    i = exchange_both(far_part(free_rows, n), f)
    operands = [v for k in range(2) for v in (*n[2 * k:2 * k + 2], *f[2 * k:2 * k + 2])]
    d = exchange_both(
        call(pass_on_kernel, weights + [near, far] + operands, [sent(128)] * 4, left_rows(256) + scales(12)), i
    )
    own = call(own_kernel, weights + [near, far], [kept(256)] * 2, left_rows(256), i)

    def stage_one_of(kind):
        return [own[kind]] + [v for part in (d, n, i) for v in part[2 * kind:2 * kind + 2]]

    got = [None, None]
    for k in range(2):
        p, q = call(functools.partial(second_opposite_kernel, k), stage_one_of(k), [sent(32)] * 2, scales(8))
        got[k] = send(p, FORWARD[1 - k]), send(q, BACKWARD[1 - k])
    for k in range(2):
        p, q = call(
            functools.partial(second_neighbour_kernel, k), stage_one_of(k) + [*got[k]], [sent(64)] * 2, scales(10)
        )
        got[k] = send(p, FORWARD[1 - k]), send(q, BACKWARD[1 - k])
    for k in range(2):
        a, b, c, rest = call(
            functools.partial(spread_kernel, k), stage_one_of(k) + [*got[k]], [sent(16)] * 3 + [floats(16)],
            [pltpu.VMEM((64, TILE), jnp.float32)] + scales(11),
        )
        got[k] = rest, send(a, ACROSS), send_col(b, 2), lax.ppermute(c, ("row", "col"), DIAGONAL)
    outs = []
    for k in range(2):
        outs.append(call(last_kernel, [*got[k]], [jax.ShapeDtypeStruct((16, width), jnp.bfloat16)] * 2, scales(3)))
    outs = [outs[k][part] for part in range(2) for k in range(2)]
    summed = jnp.concatenate(outs, axis=1).reshape(2, 8, 2 * columns)
    mine = lax.dynamic_index_in_dim(summed, core, 0, keepdims=False)
    other = send_col(lax.dynamic_index_in_dim(summed, 1 - core, 0, keepdims=False), 1)
    even, odd = jnp.where(core == 0, mine, other), jnp.where(core == 0, other, mine)
    near_pair = [even[:, :columns], odd[:, :columns]]
    far_pair = [even[:, columns:], odd[:, columns:]]
    first = [jnp.where(z_hi == 0, u, v) for u, v in zip(near_pair, far_pair)]
    last = [jnp.where(z_hi == 0, v, u) for u, v in zip(near_pair, far_pair)]
    return jnp.concatenate(first + last, axis=1)


def solution(mesh):
    in_specs = (
        P(("row", "col"), None),
        P(("row", "col"), None),
        P("row", "col"),
        P("row", "col"),
        P(),
    )
    out_specs = P(("row", "col"), None)
    return jax.shard_map(
        per_device, mesh=mesh, in_specs=in_specs, out_specs=out_specs, check_vma=False
    )
```

```python
import functools

import jax
import jax.numpy as jnp
from jax import lax
from jax.experimental import pallas as pl
from jax.experimental.pallas import tpu as pltpu
from jax.sharding import PartitionSpec as P

LEVELS = 32600.0
STEPS = 32.0
ROUNDER = 12582912.0
CODES = (32, 128)
VMEM_LIMIT = 12 * 1024 * 1024
BEGIN_LIMIT = 36 * 1024 * 1024
TILE = 896


def shift(dz, dx, dy):
    pairs = []
    for index in range(32):
        z, x, y = index // 16, (index // 4) % 4, index % 4
        pairs.append((index, ((z + dz) % 2) * 16 + ((x + dx) % 4) * 4 + (y + dy) % 4))
    return pairs


FORWARD = (shift(0, 1, 0), shift(0, 0, 1))
BACKWARD = (shift(0, -1, 0), shift(0, 0, -1))
ACROSS = shift(1, 0, 0)
DIAGONAL = [(r * 4 + c, s * 4 + (c ^ 2)) for r, s in ACROSS for c in range(4)]


def send(value, pairs):
    return lax.ppermute(value, "row", pairs)


def send_col(value, step):
    return lax.ppermute(value, "col", [(c, c ^ step) for c in range(4)])


def quantised(value):
    rows, tile = value.shape
    largest = jnp.max(jnp.max(jnp.abs(value.reshape(rows // 8, 8, tile)), axis=0), axis=0, keepdims=True)
    code = jnp.ceil(jnp.log2(jnp.maximum(largest, 1e-30)) * STEPS)
    factor = jnp.exp2(code * (-1.0 / STEPS)) * LEVELS
    rounded = (value * factor + ROUNDER) - ROUNDER
    return rounded.astype(jnp.int32).astype(jnp.int16), code


def finish(out_ref, code_ref):
    rows = out_ref.shape[0]
    codes = code_ref[...].astype(jnp.int32).astype(jnp.int16)
    if rows == 16:
        width = out_ref.shape[1] - 256
        out_ref[:, width:width + 128] = codes[:16]
        out_ref[:, width + 128:] = codes[16:]
        return
    width = out_ref.shape[1] - 128
    out_ref[:32, width:] = codes
    if rows > 32:
        out_ref[32:, width:] = jnp.zeros((rows - 32, 128), jnp.int16)


def encode(value, t, out_ref, code_ref):
    count = TILE // 128
    out_ref[:, columns_of(t)], code = quantised(value)
    for i in range(count):
        code_ref[pl.ds(t * count + i, 1), :] = code[:, i * 128:(i + 1) * 128]


def columns_of(t):
    return pl.ds(pl.multiple_of(t * TILE, 128), TILE)


def each_tile(width, unroll=1):
    return pl.loop(0, width // TILE, unroll=unroll)


def copy_rows(parts, left_ref, at, kind, first, z):
    first_stride, second_stride = (4, 1) if kind == 0 else (1, 4)
    for second in range(4):
        start = pl.multiple_of((z * 16 + second * second_stride + first * first_stride) * 16, 16)
        for part in parts:
            left_ref[at:at + 16, :] = part[pl.ds(start, 16), :]
            at += 16


def arrange_kernel(order, values, flags, tile_flags, out, flags_out, kept):
    for l in range(tile_flags.shape[1]):
        wide = jnp.broadcast_to(tile_flags[:, l:l + 1].astype(jnp.float32), (tile_flags.shape[0], 128))
        flags_out[:, l * 128:(l + 1) * 128] = wide.astype(jnp.bfloat16)
    tiles = flags.shape[1]
    for t in range(tiles):
        at = slice(t * 128, (t + 1) * 128)
        kept[:, at] = values[:, at] * flags[:, t:t + 1].astype(jnp.float32).astype(jnp.bfloat16)
    for k in range(tiles):
        out[:, k * 128:(k + 1) * 128] = kept[:, pl.ds(pl.multiple_of(order[k] * 128, 128), 128)]


def clear(*code_refs):
    for code_ref in code_refs:
        code_ref[...] = jnp.zeros(CODES, jnp.float32)


def dot(left, right):
    return jnp.dot(left, right, preferred_element_type=jnp.float32)


def opposite_rows(pos, kind, a, left, at_p, at_q):
    first = (pos[1 + kind] + 2) % 4
    copy_rows((a,), left, at_p, kind, first, 0)
    copy_rows((a,), left, at_q, kind, first, 1)


def free_rows(pos, kind, a, left, at_p, at_q):
    copy_rows((a,), left, at_p, kind, (pos[1 + kind] + 1) % 4, 1)
    copy_rows((a,), left, at_q, kind, (pos[1 + kind] + 3) % 4, 0)


def begin_kernel(pos, b, m, a, p0, q0, p1, q1, w0, w1, left, sems, *code_refs):
    tiles = w0.shape[1] // TILE

    def copy(kind, t):
        w = (w0, w1)[kind]
        at = pl.ds(kind * tiles * TILE + t * TILE, TILE)
        return pltpu.make_async_copy(b.at[:, at], w.at[:, pl.ds(t * TILE, TILE)], sems.at[kind * tiles + t])

    for t in range(tiles):
        for kind in range(2):
            copy(kind, t).start()
    clear(*code_refs)
    for kind in range(2):
        opposite_rows(pos, kind, a, left.at[kind], 0, 128)
        free_rows(pos, kind, a, left.at[kind], 64, 192)
    for t in range(tiles):
        for kind, w, p, q in ((0, w0, p0, q0), (1, w1, p1, q1)):
            copy(kind, t).wait()
            at = slice(t * TILE, (t + 1) * TILE)
            flags = m[:, (kind * tiles + t) * TILE:(kind * tiles + t + 1) * TILE]
            for k in range(w.shape[0] // 128):
                rows = slice(k * 128, (k + 1) * 128)
                w[rows, at] = w[rows, at] * flags[k:k + 1, :]
            sums = dot(left[kind], w[:, at])
            encode(sums[:128], t, p, code_refs[2 * kind])
            encode(sums[128:], t, q, code_refs[2 * kind + 1])
    for ref, code_ref in zip((p0, q0, p1, q1), code_refs):
        finish(ref, code_ref)


def far_kernel(rows, pos, w0, w1, a, p0, q0, p1, q1, left, *code_refs):
    clear(*code_refs)
    for kind, w, p, q in ((0, w0, p0, q0), (1, w1, p1, q1)):
        rows(pos, kind, a, left, 0, 64)

        @each_tile(w.shape[1], 2)
        def _(t):
            sums = dot(left[...], w[:, columns_of(t)])
            encode(sums[:64], t, p, code_refs[2 * kind])
            encode(sums[64:], t, q, code_refs[2 * kind + 1])

        finish(p, code_refs[2 * kind])
        finish(q, code_refs[2 * kind + 1])


def own_kernel(pos, w0, w1, near, far, *refs):
    got, outs, left, factor_refs = refs[:8], refs[8:10], refs[10], refs[11:]
    for ref, factor in zip(got, factor_refs):
        read_factors(ref, factor)
    for kind, w, own in ((0, w0, outs[0]), (1, w1, outs[1])):
        for z in range(2):
            copy_rows((near, far), left, z * 128, kind, pos[1 + kind], z)

        @each_tile(w.shape[1], 2)
        def _(t):
            sums = dot(left[...], w[:, columns_of(t)])
            for z in range(2):
                parts = [
                    decode(got[4 * kind + at + 1 - z], factor_refs[4 * kind + at + 1 - z], t, slice(start, start + 64))
                    for at, start in ((0, 64), (2, 0))
                ]
                value = sums[z * 128:z * 128 + 128] + mixed(*parts)
                own[z * 128:z * 128 + 128, columns_of(t)] = value


def mixed(near, far):
    return jnp.concatenate([part[at:at + 16] for at in range(0, 64, 16) for part in (near, far)], axis=0)


def read_factors(ref, factor_ref):
    if ref.shape[0] == 16:
        width = ref.shape[1] - 256
        codes = jnp.concatenate([ref[:, width:width + 128], ref[:, width + 128:]], axis=0)
    else:
        codes = ref[:32, ref.shape[1] - 128:]
    factor_ref[...] = jnp.exp2(codes.astype(jnp.int32).astype(jnp.float32) * (1.0 / STEPS)) * (1.0 / LEVELS)


def decode(ref, factor_ref, t, rows=slice(None)):
    count = TILE // 128
    scale = jnp.concatenate([factor_ref[pl.ds(t * count + i, 1), :] for i in range(count)], axis=1)
    return ref[rows, columns_of(t)].astype(jnp.int32).astype(jnp.float32) * scale


def pass_on_kernel(pos, w0, w1, near, far, *refs):
    outs, left, factor_refs, code_refs = refs[8:12], refs[12], refs[13:21], refs[21:]
    clear(*code_refs)
    for kind, w in ((0, w0), (1, w1)):
        got, scale = refs[4 * kind:4 * kind + 4], factor_refs[4 * kind:4 * kind + 4]
        copy_rows((near, far), left, 0, kind, (pos[1 + kind] + 1) % 4, 0)
        copy_rows((near, far), left, 128, kind, (pos[1 + kind] + 3) % 4, 1)
        for ref, factor in zip(got, scale):
            read_factors(ref, factor)

        @each_tile(w.shape[1], 2)
        def _(t):
            sums = dot(left[...], w[:, columns_of(t)])
            for way in range(2):
                n, f = (decode(got[2 * part + way], scale[2 * part + way], t, slice(0, 64)) for part in range(2))
                value = sums[way * 128:way * 128 + 128] + mixed(n, f)
                encode(value, t, outs[2 * kind + way], code_refs[2 * kind + way])

        for way in range(2):
            finish(outs[2 * kind + way], code_refs[2 * kind + way])


def stage_one(refs, factor_refs, second, t):
    own, *got = refs
    here = pl.ds(pl.multiple_of(second * 32, 32), 32)
    return [
        own[pl.ds(pl.multiple_of(z * 128 + second * 32, 32), 32), columns_of(t)] + decode(got[z], factor_refs[z], t, here)
        for z in range(2)
    ]


def second_opposite_kernel(kind, pos, *refs):
    some, outs, factor_refs, code_refs = refs[:3], refs[3:5], refs[5:7], refs[7:]
    clear(*code_refs)
    for ref, factor in zip(some[1:], factor_refs):
        read_factors(ref, factor)

    @each_tile(some[0].shape[1], 2)
    def _(t):
        sums = stage_one(some, factor_refs, (pos[2 - kind] + 2) % 4, t)
        for z in range(2):
            encode(sums[z], t, outs[z], code_refs[z])

    for z in range(2):
        finish(outs[z], code_refs[z])


def second_neighbour_kernel(kind, pos, *refs):
    some, got, outs, factor_refs, code_refs = refs[:3], refs[3:5], refs[5:7], refs[7:11], refs[11:]
    clear(*code_refs)
    for ref, factor in zip(refs[1:5], factor_refs):
        read_factors(ref, factor)

    @each_tile(some[0].shape[1], 2)
    def _(t):
        for way in range(2):
            sums = stage_one(some, factor_refs[:2], (pos[2 - kind] + (1 if way == 0 else 3)) % 4, t)
            sums[way] = sums[way] + decode(got[way], factor_refs[2 + way], t)
            encode(jnp.concatenate(sums, axis=0), t, outs[way], code_refs[way])

    for way in range(2):
        finish(outs[way], code_refs[way])


def spread_kernel(kind, pos, *refs):
    some, got, outs, sums, factor_refs, code_refs = refs[:3], refs[3:5], refs[5:9], refs[9], refs[10:14], refs[14:]
    clear(*code_refs)
    z = pos[0]
    for ref, factor in zip(refs[1:5], factor_refs):
        read_factors(ref, factor)

    def rows(h, far):
        return sums[pl.ds(pl.multiple_of(h * 32 + far * 16, 16), 16), :]

    @each_tile(some[0].shape[1], 2)
    def _(t):
        value = jnp.concatenate(stage_one(some, factor_refs[:2], pos[2 - kind], t), axis=0)
        sums[...] = value + decode(got[0], factor_refs[2], t) + decode(got[1], factor_refs[3], t)
        for at, (h, far) in enumerate(((1 - z, 0), (z, 1), (1 - z, 1))):
            encode(rows(h, far), t, outs[at], code_refs[at])
        outs[3][:, columns_of(t)] = rows(z, 0)

    for at in range(3):
        finish(outs[at], code_refs[at])


def last_kernel(pos, rest, a, b, c, near, far, f0, f1, f2):
    for ref, factor in ((a, f0), (b, f1), (c, f2)):
        read_factors(ref, factor)

    @each_tile(rest.shape[1], 2)
    def _(t):
        at = columns_of(t)
        near[:, at] = (rest[:, at] + decode(a, f0, t)).astype(jnp.bfloat16)
        far[:, at] = (decode(b, f1, t) + decode(c, f2, t)).astype(jnp.bfloat16)


COST = pl.CostEstimate(flops=1000, bytes_accessed=1000, transcendentals=0)


def position():
    row = lax.axis_index("row")
    return row // 16, (row // 4) % 4, row % 4


class Calls:
    def __init__(self, first):
        self.last = first

    def __call__(self, kernel, values, outs, scratch=(), after=(), in_hbm=(), limit=VMEM_LIMIT):
        after = [self.last, *after]
        skipped = len(after)
        name = kernel.func.__name__ if isinstance(kernel, functools.partial) else kernel.__name__
        vmem = pl.BlockSpec(memory_space=pltpu.VMEM)
        results = pl.pallas_call(
            lambda *refs: kernel(position(), *refs[skipped:]),
            in_specs=[pl.BlockSpec(memory_space=pl.ANY)] * skipped
            + [pl.BlockSpec(memory_space=pltpu.HBM)] * len(in_hbm) + [vmem] * len(values),
            out_specs=[vmem] * len(outs),
            out_shape=outs,
            scratch_shapes=list(scratch),
            compiler_params=pltpu.CompilerParams(vmem_limit_bytes=limit),
            cost_estimate=COST,
            name=name,
        )(*after, *in_hbm, *values)
        self.last = results[0]
        return results


def scales(count):
    return [pltpu.VMEM(CODES, jnp.float32)] * count


def per_device(amplitudes, amplitude_mask, integrals, integral_mask, tile_order):
    pair_count, full_width = amplitudes.shape
    depth, columns = integrals.shape
    width = columns // 2
    col = lax.axis_index("col")
    core, z_hi = col % 2, col // 2

    ordered, flags = pl.pallas_call(
        arrange_kernel,
        in_specs=[pl.BlockSpec(memory_space=pltpu.SMEM)] + [pl.BlockSpec(memory_space=pltpu.VMEM)] * 3,
        out_specs=[pl.BlockSpec(memory_space=pltpu.VMEM)] * 2,
        out_shape=[
            jax.ShapeDtypeStruct((pair_count, full_width), jnp.bfloat16),
            pltpu.VMEM((integral_mask.shape[0], columns), jnp.bfloat16),
        ],
        scratch_shapes=[pltpu.VMEM((pair_count, full_width), jnp.bfloat16)],
        name="arrange",
    )(tile_order, amplitudes, amplitude_mask, integral_mask)
    placed = lax.all_to_all(ordered, "row", split_axis=1, concat_axis=0, tiled=True)

    def both_cores(mine, other):
        even, odd = jnp.where(core == 0, mine, other), jnp.where(core == 0, other, mine)
        return jnp.stack([even.reshape(32, 8, depth), odd.reshape(32, 8, depth)], axis=1).reshape(512, depth)

    over = send_col(placed, 2)
    near = both_cores(placed, send_col(placed, 1))

    def sent(rows):
        return jax.ShapeDtypeStruct((rows, width + max(128, 4096 // rows)), jnp.int16)

    def floats(rows):
        return jax.ShapeDtypeStruct((rows, width), jnp.float32)

    call = Calls(placed)

    def kept(rows):
        return pltpu.VMEM((rows, width), jnp.float32)

    def left_rows(*rows):
        return [pltpu.VMEM((*rows, depth), jnp.bfloat16)]

    def exchange_both(outs, ahead=()):
        sends = []
        for k in range(2):
            p, q = outs[2 * k:2 * k + 2]
            if ahead:
                p, q, *_ = lax.optimization_barrier((p, q, *ahead[2 * k:2 * k + 2]))
            sends += [send(p, FORWARD[k]), send(q, BACKWARD[k])]
        return sends

    results = call(
        begin_kernel, [flags, near], [sent(128)] * 4 + [pltpu.VMEM((depth, width), jnp.bfloat16)] * 2,
        left_rows(2, 256) + [pltpu.SemaphoreType.DMA((columns // TILE,))] + scales(4), in_hbm=[integrals],
        limit=BEGIN_LIMIT,
    )
    n, weights = exchange_both(results[:4]), list(results[4:])
    over, _ = lax.optimization_barrier((over, call.last))
    far = both_cores(over, send_col(over, 1))

    def far_part(rows, after):
        return call(
            functools.partial(far_kernel, rows), weights + [far], [sent(64)] * 4, left_rows(128) + scales(4), after
        )

    f = exchange_both(far_part(opposite_rows, ()), n)
    i = exchange_both(far_part(free_rows, n), f)
    operands = [v for k in range(2) for v in (*n[2 * k:2 * k + 2], *f[2 * k:2 * k + 2])]
    d = exchange_both(
        call(pass_on_kernel, weights + [near, far] + operands, [sent(128)] * 4, left_rows(256) + scales(12)), i
    )
    operands = [v for k in range(2) for v in (*n[2 * k:2 * k + 2], *i[2 * k:2 * k + 2])]
    own = call(own_kernel, weights + [near, far] + operands, [kept(256)] * 2, left_rows(256) + scales(8))

    def stage_one_of(kind):
        return [own[kind], *d[2 * kind:2 * kind + 2]]

    got = [None, None]
    for k in range(2):
        p, q = call(functools.partial(second_opposite_kernel, k), stage_one_of(k), [sent(32)] * 2, scales(4))
        got[k] = send(p, FORWARD[1 - k]), send(q, BACKWARD[1 - k])
    for k in range(2):
        p, q = call(
            functools.partial(second_neighbour_kernel, k), stage_one_of(k) + [*got[k]], [sent(64)] * 2, scales(6)
        )
        got[k] = send(p, FORWARD[1 - k]), send(q, BACKWARD[1 - k])
    for k in range(2):
        a, b, c, rest = call(
            functools.partial(spread_kernel, k), stage_one_of(k) + [*got[k]], [sent(16)] * 3 + [floats(16)],
            [pltpu.VMEM((64, TILE), jnp.float32)] + scales(7),
        )
        b, c = send_col(b, 2), lax.ppermute(c, ("row", "col"), DIAGONAL)
        got[k] = rest, send(a, ACROSS), b, c
    outs = []
    for k in range(2):
        outs.append(call(last_kernel, [*got[k]], [jax.ShapeDtypeStruct((16, width), jnp.bfloat16)] * 2, scales(3)))
    outs = [outs[k][part] for part in range(2) for k in range(2)]
    summed = jnp.concatenate(outs, axis=1).reshape(2, 8, 2 * columns)
    mine = lax.dynamic_index_in_dim(summed, core, 0, keepdims=False)
    other = send_col(lax.dynamic_index_in_dim(summed, 1 - core, 0, keepdims=False), 1)
    even, odd = jnp.where(core == 0, mine, other), jnp.where(core == 0, other, mine)
    near_pair = [even[:, :columns], odd[:, :columns]]
    far_pair = [even[:, columns:], odd[:, columns:]]
    first = [jnp.where(z_hi == 0, u, v) for u, v in zip(near_pair, far_pair)]
    last = [jnp.where(z_hi == 0, v, u) for u, v in zip(near_pair, far_pair)]
    return jnp.concatenate(first + last, axis=1)


def solution(mesh):
    in_specs = (
        P(("row", "col"), None),
        P(("row", "col"), None),
        P("row", "col"),
        P("row", "col"),
        P(),
    )
    out_specs = P(("row", "col"), None)
    return jax.shard_map(
        per_device, mesh=mesh, in_specs=in_specs, out_specs=out_specs, check_vma=False
    )
```

```python
import functools

import jax
import jax.numpy as jnp
from jax import lax
from jax.experimental import pallas as pl
from jax.experimental.pallas import tpu as pltpu
from jax.sharding import PartitionSpec as P

LEVELS = 32600.0
STEPS = 32.0
ROUNDER = 12582912.0
CODES = (32, 128)
VMEM_LIMIT = 12 * 1024 * 1024
BEGIN_LIMIT = 36 * 1024 * 1024
TILE = 896
WIDTH_TILES = 28


def shift(dz, dx, dy):
    pairs = []
    for index in range(32):
        z, x, y = index // 16, (index // 4) % 4, index % 4
        pairs.append((index, ((z + dz) % 2) * 16 + ((x + dx) % 4) * 4 + (y + dy) % 4))
    return pairs


FORWARD = (shift(0, 1, 0), shift(0, 0, 1))
BACKWARD = (shift(0, -1, 0), shift(0, 0, -1))
ACROSS = shift(1, 0, 0)
DIAGONAL = [(r * 4 + c, s * 4 + (c ^ 2)) for r, s in ACROSS for c in range(4)]


def send(value, pairs):
    return lax.ppermute(value, "row", pairs)


def send_col(value, step):
    return lax.ppermute(value, "col", [(c, c ^ step) for c in range(4)])


def quantised(value):
    rows, tile = value.shape
    largest = jnp.max(jnp.max(jnp.abs(value.reshape(rows // 8, 8, tile)), axis=0), axis=0, keepdims=True)
    code = jnp.ceil(jnp.log2(jnp.maximum(largest, 1e-30)) * STEPS)
    factor = jnp.exp2(code * (-1.0 / STEPS)) * LEVELS
    rounded = (value * factor + ROUNDER) - ROUNDER
    return rounded.astype(jnp.int32).astype(jnp.int16), code


def finish(out_ref, code_ref):
    out_ref[out_ref.shape[0] - 32:, :] = code_ref[...].astype(jnp.int32).astype(jnp.int16)


def encode(value, t, out_ref, code_ref):
    count, rows = TILE // 128, value.shape[0]
    coded, code = quantised(value)
    for i in range(count):
        at = t * count + i
        out_ref[pl.ds(pl.multiple_of(at * rows, 16), rows), :] = coded[:, i * 128:(i + 1) * 128]
        code_ref[pl.ds(at, 1), :] = code[:, i * 128:(i + 1) * 128]


def columns_of(t):
    return pl.ds(pl.multiple_of(t * TILE, 128), TILE)


def each_tile(width, unroll=1):
    return pl.loop(0, width // TILE, unroll=unroll)


def copy_rows(parts, left_ref, at, kind, first, z):
    first_stride, second_stride = (4, 1) if kind == 0 else (1, 4)
    for second in range(4):
        start = pl.multiple_of((z * 16 + second * second_stride + first * first_stride) * 16, 16)
        for part in parts:
            left_ref[at:at + 16, :] = part[pl.ds(start, 16), :]
            at += 16


def arrange_kernel(order, values, flags, tile_flags, out, flags_out, kept):
    for l in range(tile_flags.shape[1]):
        wide = jnp.broadcast_to(tile_flags[:, l:l + 1].astype(jnp.float32), (tile_flags.shape[0], 128))
        flags_out[:, l * 128:(l + 1) * 128] = wide.astype(jnp.bfloat16)
    tiles = flags.shape[1]
    for t in range(tiles):
        at = slice(t * 128, (t + 1) * 128)
        kept[:, at] = values[:, at] * flags[:, t:t + 1].astype(jnp.float32).astype(jnp.bfloat16)
    for k in range(tiles):
        out[:, k * 128:(k + 1) * 128] = kept[:, pl.ds(pl.multiple_of(order[k] * 128, 128), 128)]


def clear(*code_refs):
    for code_ref in code_refs:
        code_ref[...] = jnp.zeros(CODES, jnp.float32)


def dot(left, right):
    return jnp.dot(left, right, preferred_element_type=jnp.float32)


def opposite_rows(pos, kind, a, left, at_p, at_q):
    first = (pos[1 + kind] + 2) % 4
    copy_rows((a,), left, at_p, kind, first, 0)
    copy_rows((a,), left, at_q, kind, first, 1)


def free_rows(pos, kind, a, left, at_p, at_q):
    copy_rows((a,), left, at_p, kind, (pos[1 + kind] + 1) % 4, 1)
    copy_rows((a,), left, at_q, kind, (pos[1 + kind] + 3) % 4, 0)


def begin_kernel(pos, b, m, a, p0, q0, p1, q1, w0, w1, left, sems, *code_refs):
    tiles = w0.shape[1] // TILE

    def copy(kind, t):
        w = (w0, w1)[kind]
        at = pl.ds(kind * tiles * TILE + t * TILE, TILE)
        return pltpu.make_async_copy(b.at[:, at], w.at[:, pl.ds(t * TILE, TILE)], sems.at[kind * tiles + t])

    for t in range(tiles):
        for kind in range(2):
            copy(kind, t).start()
    clear(*code_refs)
    for kind in range(2):
        opposite_rows(pos, kind, a, left.at[kind], 0, 128)
        free_rows(pos, kind, a, left.at[kind], 64, 192)
    for t in range(tiles):
        for kind, w, p, q in ((0, w0, p0, q0), (1, w1, p1, q1)):
            copy(kind, t).wait()
            at = slice(t * TILE, (t + 1) * TILE)
            flags = m[:, (kind * tiles + t) * TILE:(kind * tiles + t + 1) * TILE]
            for k in range(w.shape[0] // 128):
                rows = slice(k * 128, (k + 1) * 128)
                w[rows, at] = w[rows, at] * flags[k:k + 1, :]
            sums = dot(left[kind], w[:, at])
            encode(sums[:128], t, p, code_refs[2 * kind])
            encode(sums[128:], t, q, code_refs[2 * kind + 1])
    for ref, code_ref in zip((p0, q0, p1, q1), code_refs):
        finish(ref, code_ref)


def far_kernel(pos, w0, w1, a, p0, q0, p1, q1, left, *code_refs):
    clear(*code_refs)
    for kind, w, p, q in ((0, w0, p0, q0), (1, w1, p1, q1)):
        opposite_rows(pos, kind, a, left, 0, 128)
        free_rows(pos, kind, a, left, 64, 192)

        @each_tile(w.shape[1], 2)
        def _(t):
            sums = dot(left[...], w[:, columns_of(t)])
            encode(sums[:128], t, p, code_refs[2 * kind])
            encode(sums[128:], t, q, code_refs[2 * kind + 1])

        finish(p, code_refs[2 * kind])
        finish(q, code_refs[2 * kind + 1])


def own_kernel(pos, w0, w1, near, far, *refs):
    got, outs, left, factor_refs = refs[:8], refs[8:10], refs[10], refs[11:]
    for ref, factor in zip(got, factor_refs):
        read_factors(ref, factor)
    for kind, w, own in ((0, w0, outs[0]), (1, w1, outs[1])):
        for z in range(2):
            copy_rows((near, far), left, z * 128, kind, pos[1 + kind], z)

        @each_tile(w.shape[1], 2)
        def _(t):
            sums = dot(left[...], w[:, columns_of(t)])
            for z in range(2):
                parts = [
                    decode(got[4 * kind + at + 1 - z], factor_refs[4 * kind + at + 1 - z], t, 64, 64)
                    for at in (0, 2)
                ]
                value = sums[z * 128:z * 128 + 128] + mixed(*parts)
                own[z * 128:z * 128 + 128, columns_of(t)] = value


def mixed(near, far):
    return jnp.concatenate([part[at:at + 16] for at in range(0, 64, 16) for part in (near, far)], axis=0)


def read_factors(ref, factor_ref):
    codes = ref[ref.shape[0] - 32:, :].astype(jnp.int32).astype(jnp.float32)
    factor_ref[...] = jnp.exp2(codes * (1.0 / STEPS)) * (1.0 / LEVELS)


def decode(ref, factor_ref, t, start=0, size=None):
    count, rows = TILE // 128, (ref.shape[0] - 32) // WIDTH_TILES
    parts = []
    for i in range(count):
        at = t * count + i
        part = ref[pl.ds(pl.multiple_of(at * rows + start, 16), size or rows), :]
        parts.append(part.astype(jnp.int32).astype(jnp.float32) * factor_ref[pl.ds(at, 1), :])
    return jnp.concatenate(parts, axis=1)


def later_kernel(pos, w0, w1, near, far, *refs):
    got, outs, left, factor_refs = refs[:4], refs[4:6], refs[6], refs[7:]
    for ref, factor in zip(got, factor_refs):
        read_factors(ref, factor)
    for kind, w, out in ((0, w0, outs[0]), (1, w1, outs[1])):
        copy_rows((near, far), left, 0, kind, (pos[1 + kind] + 1) % 4, 0)
        copy_rows((near, far), left, 128, kind, (pos[1 + kind] + 3) % 4, 1)

        @each_tile(w.shape[1], 2)
        def _(t):
            sums = dot(left[...], w[:, columns_of(t)])
            for way in range(2):
                n = decode(got[2 * kind + way], factor_refs[2 * kind + way], t, 0, 64)
                out[way * 128:way * 128 + 128, columns_of(t)] = sums[way * 128:way * 128 + 128] + mixed(n, jnp.zeros_like(n))


def pass_on_kernel(pos, later, p, q, *refs):
    outs, factor_refs, code_refs = refs[:2], refs[2:4], refs[4:]
    clear(*code_refs)
    for ref, factor in zip((p, q), factor_refs):
        read_factors(ref, factor)

    @each_tile(later.shape[1], 2)
    def _(t):
        for way, ref in enumerate((p, q)):
            f = decode(ref, factor_refs[way], t, 0, 64)
            value = later[way * 128:way * 128 + 128, columns_of(t)] + mixed(jnp.zeros_like(f), f)
            encode(value, t, outs[way], code_refs[way])

    for way in range(2):
        finish(outs[way], code_refs[way])


def stage_one(refs, factor_refs, second, t):
    own, *got = refs
    return [
        own[pl.ds(pl.multiple_of(z * 128 + second * 32, 32), 32), columns_of(t)] + decode(got[z], factor_refs[z], t, second * 32, 32)
        for z in range(2)
    ]


def second_opposite_kernel(kind, pos, *refs):
    some, outs, factor_refs, code_refs = refs[:3], refs[3:5], refs[5:7], refs[7:]
    clear(*code_refs)
    for ref, factor in zip(some[1:], factor_refs):
        read_factors(ref, factor)

    @each_tile(some[0].shape[1], 2)
    def _(t):
        sums = stage_one(some, factor_refs, (pos[2 - kind] + 2) % 4, t)
        for z in range(2):
            encode(sums[z], t, outs[z], code_refs[z])

    for z in range(2):
        finish(outs[z], code_refs[z])


def second_neighbour_kernel(kind, pos, *refs):
    some, got, outs, factor_refs, code_refs = refs[:3], refs[3:5], refs[5:7], refs[7:11], refs[11:]
    clear(*code_refs)
    for ref, factor in zip(refs[1:5], factor_refs):
        read_factors(ref, factor)

    @each_tile(some[0].shape[1], 2)
    def _(t):
        for way in range(2):
            sums = stage_one(some, factor_refs[:2], (pos[2 - kind] + (1 if way == 0 else 3)) % 4, t)
            sums[way] = sums[way] + decode(got[way], factor_refs[2 + way], t)
            encode(jnp.concatenate(sums, axis=0), t, outs[way], code_refs[way])

    for way in range(2):
        finish(outs[way], code_refs[way])


def spread_kernel(kind, pos, *refs):
    some, got, outs, sums, factor_refs, code_refs = refs[:3], refs[3:5], refs[5:9], refs[9], refs[10:14], refs[14:]
    clear(*code_refs)
    z = pos[0]
    for ref, factor in zip(refs[1:5], factor_refs):
        read_factors(ref, factor)

    def rows(h, far):
        return sums[pl.ds(pl.multiple_of(h * 32 + far * 16, 16), 16), :]

    @each_tile(some[0].shape[1], 2)
    def _(t):
        value = jnp.concatenate(stage_one(some, factor_refs[:2], pos[2 - kind], t), axis=0)
        sums[...] = value + decode(got[0], factor_refs[2], t) + decode(got[1], factor_refs[3], t)
        for at, (h, far) in enumerate(((1 - z, 0), (z, 1), (1 - z, 1))):
            encode(rows(h, far), t, outs[at], code_refs[at])
        outs[3][:, columns_of(t)] = rows(z, 0)

    for at in range(3):
        finish(outs[at], code_refs[at])


def last_kernel(pos, rest, a, b, c, near, far, f0, f1, f2):
    for ref, factor in ((a, f0), (b, f1), (c, f2)):
        read_factors(ref, factor)

    @each_tile(rest.shape[1], 2)
    def _(t):
        at = columns_of(t)
        near[:, at] = (rest[:, at] + decode(a, f0, t)).astype(jnp.bfloat16)
        far[:, at] = (decode(b, f1, t) + decode(c, f2, t)).astype(jnp.bfloat16)


COST = pl.CostEstimate(flops=1000, bytes_accessed=1000, transcendentals=0)


def position():
    row = lax.axis_index("row")
    return row // 16, (row // 4) % 4, row % 4


class Calls:
    def __init__(self, first):
        self.last = first

    def __call__(self, kernel, values, outs, scratch=(), after=(), in_hbm=(), limit=VMEM_LIMIT):
        after = [self.last, *after]
        skipped = len(after)
        name = kernel.func.__name__ if isinstance(kernel, functools.partial) else kernel.__name__
        vmem = pl.BlockSpec(memory_space=pltpu.VMEM)
        results = pl.pallas_call(
            lambda *refs: kernel(position(), *refs[skipped:]),
            in_specs=[pl.BlockSpec(memory_space=pl.ANY)] * skipped
            + [pl.BlockSpec(memory_space=pltpu.HBM)] * len(in_hbm) + [vmem] * len(values),
            out_specs=[vmem] * len(outs),
            out_shape=outs,
            scratch_shapes=list(scratch),
            compiler_params=pltpu.CompilerParams(vmem_limit_bytes=limit),
            cost_estimate=COST,
            name=name,
        )(*after, *in_hbm, *values)
        self.last = results[0]
        return results


def scales(count):
    return [pltpu.VMEM(CODES, jnp.float32)] * count


def per_device(amplitudes, amplitude_mask, integrals, integral_mask, tile_order):
    pair_count, full_width = amplitudes.shape
    depth, columns = integrals.shape
    width = columns // 2
    col = lax.axis_index("col")
    core, z_hi = col % 2, col // 2

    ordered, flags = pl.pallas_call(
        arrange_kernel,
        in_specs=[pl.BlockSpec(memory_space=pltpu.SMEM)] + [pl.BlockSpec(memory_space=pltpu.VMEM)] * 3,
        out_specs=[pl.BlockSpec(memory_space=pltpu.VMEM)] * 2,
        out_shape=[
            jax.ShapeDtypeStruct((pair_count, full_width), jnp.bfloat16),
            pltpu.VMEM((integral_mask.shape[0], columns), jnp.bfloat16),
        ],
        scratch_shapes=[pltpu.VMEM((pair_count, full_width), jnp.bfloat16)],
        name="arrange",
    )(tile_order, amplitudes, amplitude_mask, integral_mask)
    placed = lax.all_to_all(ordered, "row", split_axis=1, concat_axis=0, tiled=True)

    def both_cores(mine, other):
        even, odd = jnp.where(core == 0, mine, other), jnp.where(core == 0, other, mine)
        return jnp.stack([even.reshape(32, 8, depth), odd.reshape(32, 8, depth)], axis=1).reshape(512, depth)

    over = send_col(placed, 2)
    near = both_cores(placed, send_col(placed, 1))

    def sent(rows):
        return jax.ShapeDtypeStruct((WIDTH_TILES * rows + 32, 128), jnp.int16)

    def floats(rows):
        return jax.ShapeDtypeStruct((rows, width), jnp.float32)

    call = Calls(placed)

    def kept(rows):
        return pltpu.VMEM((rows, width), jnp.float32)

    def left_rows(*rows):
        return [pltpu.VMEM((*rows, depth), jnp.bfloat16)]

    def exchange_both(outs, ahead=()):
        sends = []
        for k in range(2):
            p, q = outs[2 * k:2 * k + 2]
            if ahead:
                p, q, *_ = lax.optimization_barrier((p, q, *ahead[2 * k:2 * k + 2]))
            sends += [send(p, FORWARD[k]), send(q, BACKWARD[k])]
        return sends

    results = call(
        begin_kernel, [flags, near], [sent(128)] * 4 + [pltpu.VMEM((depth, width), jnp.bfloat16)] * 2,
        left_rows(2, 256) + [pltpu.SemaphoreType.DMA((columns // TILE,))] + scales(4), in_hbm=[integrals],
        limit=BEGIN_LIMIT,
    )
    n, weights = exchange_both(results[:4]), list(results[4:])
    over, _ = lax.optimization_barrier((over, call.last))
    far = both_cores(over, send_col(over, 1))

    f = exchange_both(call(far_kernel, weights + [far], [sent(128)] * 4, left_rows(256) + scales(4)), n)
    later = call(later_kernel, weights + [near, far, *n], [kept(256)] * 2, left_rows(256) + scales(4))
    d = []
    for k in range(2):
        p, q = call(pass_on_kernel, [later[k], *f[2 * k:2 * k + 2]], [sent(128)] * 2, scales(4))
        d += [send(p, FORWARD[k]), send(q, BACKWARD[k])]
    operands = [v for k in range(2) for v in (*n[2 * k:2 * k + 2], *f[2 * k:2 * k + 2])]
    own = call(own_kernel, weights + [near, far] + operands, [kept(256)] * 2, left_rows(256) + scales(8))

    def stage_one_of(kind):
        return [own[kind], *d[2 * kind:2 * kind + 2]]

    got = [None, None]
    for k in range(2):
        p, q = call(functools.partial(second_opposite_kernel, k), stage_one_of(k), [sent(32)] * 2, scales(4))
        got[k] = send(p, FORWARD[1 - k]), send(q, BACKWARD[1 - k])
    for k in range(2):
        p, q = call(
            functools.partial(second_neighbour_kernel, k), stage_one_of(k) + [*got[k]], [sent(64)] * 2, scales(6)
        )
        got[k] = send(p, FORWARD[1 - k]), send(q, BACKWARD[1 - k])
    for k in range(2):
        a, b, c, rest = call(
            functools.partial(spread_kernel, k), stage_one_of(k) + [*got[k]], [sent(16)] * 3 + [floats(16)],
            [pltpu.VMEM((64, TILE), jnp.float32)] + scales(7),
        )
        b, c = send_col(b, 2), lax.ppermute(c, ("row", "col"), DIAGONAL)
        got[k] = rest, send(a, ACROSS), b, c
    outs = []
    for k in range(2):
        outs.append(call(last_kernel, [*got[k]], [jax.ShapeDtypeStruct((16, width), jnp.bfloat16)] * 2, scales(3)))
    outs = [outs[k][part] for part in range(2) for k in range(2)]
    summed = jnp.concatenate(outs, axis=1).reshape(2, 8, 2 * columns)
    mine = lax.dynamic_index_in_dim(summed, core, 0, keepdims=False)
    other = send_col(lax.dynamic_index_in_dim(summed, 1 - core, 0, keepdims=False), 1)
    even, odd = jnp.where(core == 0, mine, other), jnp.where(core == 0, other, mine)
    near_pair = [even[:, :columns], odd[:, :columns]]
    far_pair = [even[:, columns:], odd[:, columns:]]
    first = [jnp.where(z_hi == 0, u, v) for u, v in zip(near_pair, far_pair)]
    last = [jnp.where(z_hi == 0, v, u) for u, v in zip(near_pair, far_pair)]
    return jnp.concatenate(first + last, axis=1)


def solution(mesh):
    in_specs = (
        P(("row", "col"), None),
        P(("row", "col"), None),
        P("row", "col"),
        P("row", "col"),
        P(),
    )
    out_specs = P(("row", "col"), None)
    return jax.shard_map(
        per_device, mesh=mesh, in_specs=in_specs, out_specs=out_specs, check_vma=False
    )
```

```python
import functools

import jax
import jax.numpy as jnp
from jax import lax
from jax.experimental import pallas as pl
from jax.experimental.pallas import tpu as pltpu
from jax.sharding import PartitionSpec as P

LEVELS = 32600.0
STEPS = 32.0
ROUNDER = 12582912.0
CODES = (32, 128)
VMEM_LIMIT = 12 * 1024 * 1024
BEGIN_LIMIT = 36 * 1024 * 1024
TILE = 896
FIRST_TILE = 896
WIDTH_TILES = 28


def shift(dz, dx, dy):
    pairs = []
    for index in range(32):
        z, x, y = index // 16, (index // 4) % 4, index % 4
        pairs.append((index, ((z + dz) % 2) * 16 + ((x + dx) % 4) * 4 + (y + dy) % 4))
    return pairs


FORWARD = (shift(0, 1, 0), shift(0, 0, 1))
BACKWARD = (shift(0, -1, 0), shift(0, 0, -1))
ACROSS = shift(1, 0, 0)
DIAGONAL = [(r * 4 + c, s * 4 + (c ^ 2)) for r, s in ACROSS for c in range(4)]


def send(value, pairs):
    return lax.ppermute(value, "row", pairs)


def send_col(value, step):
    return lax.ppermute(value, "col", [(c, c ^ step) for c in range(4)])


def quantised(value):
    rows, tile = value.shape
    largest = jnp.max(jnp.max(jnp.abs(value.reshape(rows // 8, 8, tile)), axis=0), axis=0, keepdims=True)
    code = jnp.ceil(jnp.log2(jnp.maximum(largest, 1e-30)) * STEPS)
    factor = jnp.exp2(code * (-1.0 / STEPS)) * LEVELS
    rounded = (value * factor + ROUNDER) - ROUNDER
    return rounded.astype(jnp.int32).astype(jnp.int16), code


def finish(out_ref, code_ref):
    out_ref[out_ref.shape[0] - 32:, :] = code_ref[...].astype(jnp.int32).astype(jnp.int16)


def encode(value, t, out_ref, code_ref):
    count, rows = value.shape[1] // 128, value.shape[0]
    coded, code = quantised(value)
    for i in range(count):
        at = t * count + i
        out_ref[pl.ds(pl.multiple_of(at * rows, 16), rows), :] = coded[:, i * 128:(i + 1) * 128]
        code_ref[pl.ds(at, 1), :] = code[:, i * 128:(i + 1) * 128]


def columns_of(t):
    return pl.ds(pl.multiple_of(t * TILE, 128), TILE)


def each_tile(width, unroll=1):
    return pl.loop(0, width // TILE, unroll=unroll)


def copy_rows(parts, left_ref, at, kind, first, z):
    first_stride, second_stride = (4, 1) if kind == 0 else (1, 4)
    for second in range(4):
        start = pl.multiple_of((z * 16 + second * second_stride + first * first_stride) * 16, 16)
        for part in parts:
            left_ref[at:at + 16, :] = part[pl.ds(start, 16), :]
            at += 16


def arrange_kernel(order, values, flags, out, kept):
    tiles = flags.shape[1]
    for t in range(tiles):
        at = slice(t * 128, (t + 1) * 128)
        kept[:, at] = values[:, at] * flags[:, t:t + 1].astype(jnp.float32).astype(jnp.bfloat16)
    for k in range(tiles):
        out[:, k * 128:(k + 1) * 128] = kept[:, pl.ds(pl.multiple_of(order[k] * 128, 128), 128)]


def clear(*code_refs):
    for code_ref in code_refs:
        code_ref[...] = jnp.zeros(CODES, jnp.float32)


def dot(left, right):
    return jnp.dot(left, right, preferred_element_type=jnp.float32)


def opposite_rows(pos, kind, a, left, at_p, at_q):
    first = (pos[1 + kind] + 2) % 4
    copy_rows((a,), left, at_p, kind, first, 0)
    copy_rows((a,), left, at_q, kind, first, 1)


def free_rows(pos, kind, a, left, at_p, at_q):
    copy_rows((a,), left, at_p, kind, (pos[1 + kind] + 1) % 4, 1)
    copy_rows((a,), left, at_q, kind, (pos[1 + kind] + 3) % 4, 0)


def begin_kernel(pos, b, m, a, p0, q0, p1, q1, w0, w1, left, wide, sems, *code_refs):
    tiles = w0.shape[1] // FIRST_TILE

    def copy(kind, t):
        w = (w0, w1)[kind]
        at = pl.ds(kind * tiles * FIRST_TILE + t * FIRST_TILE, FIRST_TILE)
        return pltpu.make_async_copy(b.at[:, at], w.at[:, pl.ds(t * FIRST_TILE, FIRST_TILE)], sems.at[kind * tiles + t])

    for t in range(tiles):
        for kind in range(2):
            copy(kind, t).start()
    for l in range(m.shape[1]):
        wide[:, l * 128:(l + 1) * 128] = jnp.broadcast_to(m[:, l:l + 1].astype(jnp.float32), (m.shape[0], 128))
    clear(*code_refs)
    for kind in range(2):
        opposite_rows(pos, kind, a, left.at[kind], 0, 128)
        free_rows(pos, kind, a, left.at[kind], 64, 192)
    for t in range(tiles):
        for kind, w, p, q in ((0, w0, p0, q0), (1, w1, p1, q1)):
            copy(kind, t).wait()
            at = slice(t * FIRST_TILE, (t + 1) * FIRST_TILE)
            flags = wide[:, (kind * tiles + t) * FIRST_TILE:(kind * tiles + t + 1) * FIRST_TILE].astype(jnp.bfloat16)
            for k in range(w.shape[0] // 128):
                rows = slice(k * 128, (k + 1) * 128)
                w[rows, at] = w[rows, at] * flags[k:k + 1, :]
            sums = dot(left[kind], w[:, at])
            encode(sums[:128], t, p, code_refs[2 * kind])
            encode(sums[128:], t, q, code_refs[2 * kind + 1])
    for ref, code_ref in zip((p0, q0, p1, q1), code_refs):
        finish(ref, code_ref)


def far_kernel(pos, w0, w1, a, p0, q0, p1, q1, left, *code_refs):
    clear(*code_refs)
    for kind, w, p, q in ((0, w0, p0, q0), (1, w1, p1, q1)):
        opposite_rows(pos, kind, a, left, 0, 128)
        free_rows(pos, kind, a, left, 64, 192)

        @each_tile(w.shape[1], 2)
        def _(t):
            sums = dot(left[...], w[:, columns_of(t)])
            encode(sums[:128], t, p, code_refs[2 * kind])
            encode(sums[128:], t, q, code_refs[2 * kind + 1])

        finish(p, code_refs[2 * kind])
        finish(q, code_refs[2 * kind + 1])


def own_kernel(pos, w0, w1, near, far, *refs):
    got, outs, left, factor_refs = refs[:8], refs[8:10], refs[10], refs[11:]
    for ref, factor in zip(got, factor_refs):
        read_factors(ref, factor)
    for kind, w, own in ((0, w0, outs[0]), (1, w1, outs[1])):
        for z in range(2):
            copy_rows((near, far), left, z * 128, kind, pos[1 + kind], z)

        @each_tile(w.shape[1], 2)
        def _(t):
            sums = dot(left[...], w[:, columns_of(t)])
            for z in range(2):
                parts = [
                    decode(got[4 * kind + at + 1 - z], factor_refs[4 * kind + at + 1 - z], t, 64, 64)
                    for at in (0, 2)
                ]
                value = sums[z * 128:z * 128 + 128] + mixed(*parts)
                own[z * 128:z * 128 + 128, columns_of(t)] = value


def mixed(near, far):
    return jnp.concatenate([part[at:at + 16] for at in range(0, 64, 16) for part in (near, far)], axis=0)


def read_factors(ref, factor_ref):
    codes = ref[ref.shape[0] - 32:, :].astype(jnp.int32).astype(jnp.float32)
    factor_ref[...] = jnp.exp2(codes * (1.0 / STEPS)) * (1.0 / LEVELS)


def decode(ref, factor_ref, t, start=0, size=None):
    count, rows = TILE // 128, (ref.shape[0] - 32) // WIDTH_TILES
    parts = []
    for i in range(count):
        at = t * count + i
        part = ref[pl.ds(pl.multiple_of(at * rows + start, 16), size or rows), :]
        parts.append(part.astype(jnp.int32).astype(jnp.float32) * factor_ref[pl.ds(at, 1), :])
    return jnp.concatenate(parts, axis=1)


def later_kernel(pos, w0, w1, near, far, *refs):
    got, outs, left, factor_refs = refs[:4], refs[4:6], refs[6], refs[7:]
    for ref, factor in zip(got, factor_refs):
        read_factors(ref, factor)
    for kind, w, out in ((0, w0, outs[0]), (1, w1, outs[1])):
        copy_rows((near, far), left, 0, kind, (pos[1 + kind] + 1) % 4, 0)
        copy_rows((near, far), left, 128, kind, (pos[1 + kind] + 3) % 4, 1)

        @each_tile(w.shape[1], 2)
        def _(t):
            sums = dot(left[...], w[:, columns_of(t)])
            for way in range(2):
                n = decode(got[2 * kind + way], factor_refs[2 * kind + way], t, 0, 64)
                out[way * 128:way * 128 + 128, columns_of(t)] = sums[way * 128:way * 128 + 128] + mixed(n, jnp.zeros_like(n))


def pass_on_kernel(pos, later, p, q, *refs):
    outs, factor_refs, code_refs = refs[:2], refs[2:4], refs[4:]
    clear(*code_refs)
    for ref, factor in zip((p, q), factor_refs):
        read_factors(ref, factor)

    @each_tile(later.shape[1], 2)
    def _(t):
        for way, ref in enumerate((p, q)):
            f = decode(ref, factor_refs[way], t, 0, 64)
            value = later[way * 128:way * 128 + 128, columns_of(t)] + mixed(jnp.zeros_like(f), f)
            encode(value, t, outs[way], code_refs[way])

    for way in range(2):
        finish(outs[way], code_refs[way])


def stage_one(refs, factor_refs, second, t):
    own, *got = refs
    return [
        own[pl.ds(pl.multiple_of(z * 128 + second * 32, 32), 32), columns_of(t)] + decode(got[z], factor_refs[z], t, second * 32, 32)
        for z in range(2)
    ]


def second_opposite_kernel(kind, pos, *refs):
    some, outs, factor_refs, code_refs = refs[:3], refs[3:5], refs[5:7], refs[7:]
    clear(*code_refs)
    for ref, factor in zip(some[1:], factor_refs):
        read_factors(ref, factor)

    @each_tile(some[0].shape[1], 2)
    def _(t):
        sums = stage_one(some, factor_refs, (pos[2 - kind] + 2) % 4, t)
        for z in range(2):
            encode(sums[z], t, outs[z], code_refs[z])

    for z in range(2):
        finish(outs[z], code_refs[z])


def second_neighbour_kernel(kind, pos, *refs):
    some, got, outs, factor_refs, code_refs = refs[:3], refs[3:5], refs[5:7], refs[7:11], refs[11:]
    clear(*code_refs)
    for ref, factor in zip(refs[1:5], factor_refs):
        read_factors(ref, factor)

    @each_tile(some[0].shape[1], 2)
    def _(t):
        for way in range(2):
            sums = stage_one(some, factor_refs[:2], (pos[2 - kind] + (1 if way == 0 else 3)) % 4, t)
            sums[way] = sums[way] + decode(got[way], factor_refs[2 + way], t)
            encode(jnp.concatenate(sums, axis=0), t, outs[way], code_refs[way])

    for way in range(2):
        finish(outs[way], code_refs[way])


def spread_kernel(kind, pos, *refs):
    some, got, outs, sums, factor_refs, code_refs = refs[:3], refs[3:5], refs[5:9], refs[9], refs[10:14], refs[14:]
    clear(*code_refs)
    z = pos[0]
    for ref, factor in zip(refs[1:5], factor_refs):
        read_factors(ref, factor)

    def rows(h, far):
        return sums[pl.ds(pl.multiple_of(h * 32 + far * 16, 16), 16), :]

    @each_tile(some[0].shape[1], 2)
    def _(t):
        value = jnp.concatenate(stage_one(some, factor_refs[:2], pos[2 - kind], t), axis=0)
        sums[...] = value + decode(got[0], factor_refs[2], t) + decode(got[1], factor_refs[3], t)
        for at, (h, far) in enumerate(((1 - z, 0), (z, 1), (1 - z, 1))):
            encode(rows(h, far), t, outs[at], code_refs[at])
        outs[3][:, columns_of(t)] = rows(z, 0)

    for at in range(3):
        finish(outs[at], code_refs[at])


def last_kernel(pos, rest, a, b, c, near, far, f0, f1, f2):
    for ref, factor in ((a, f0), (b, f1), (c, f2)):
        read_factors(ref, factor)

    @each_tile(rest.shape[1], 2)
    def _(t):
        at = columns_of(t)
        near[:, at] = (rest[:, at] + decode(a, f0, t)).astype(jnp.bfloat16)
        far[:, at] = (decode(b, f1, t) + decode(c, f2, t)).astype(jnp.bfloat16)


COST = pl.CostEstimate(flops=1000, bytes_accessed=1000, transcendentals=0)


def position():
    row = lax.axis_index("row")
    return row // 16, (row // 4) % 4, row % 4


class Calls:
    def __init__(self, first):
        self.last = first

    def __call__(self, kernel, values, outs, scratch=(), after=(), in_hbm=(), limit=VMEM_LIMIT):
        after = [self.last, *after]
        skipped = len(after)
        name = kernel.func.__name__ if isinstance(kernel, functools.partial) else kernel.__name__
        vmem = pl.BlockSpec(memory_space=pltpu.VMEM)
        results = pl.pallas_call(
            lambda *refs: kernel(position(), *refs[skipped:]),
            in_specs=[pl.BlockSpec(memory_space=pl.ANY)] * skipped
            + [pl.BlockSpec(memory_space=pltpu.HBM)] * len(in_hbm) + [vmem] * len(values),
            out_specs=[vmem] * len(outs),
            out_shape=outs,
            scratch_shapes=list(scratch),
            compiler_params=pltpu.CompilerParams(vmem_limit_bytes=limit),
            cost_estimate=COST,
            name=name,
        )(*after, *in_hbm, *values)
        self.last = results[0]
        return results


def scales(count):
    return [pltpu.VMEM(CODES, jnp.float32)] * count


def per_device(amplitudes, amplitude_mask, integrals, integral_mask, tile_order):
    pair_count, full_width = amplitudes.shape
    depth, columns = integrals.shape
    width = columns // 2
    col = lax.axis_index("col")
    core, z_hi = col % 2, col // 2

    ordered = pl.pallas_call(
        arrange_kernel,
        in_specs=[pl.BlockSpec(memory_space=pltpu.SMEM)] + [pl.BlockSpec(memory_space=pltpu.VMEM)] * 2,
        out_specs=pl.BlockSpec(memory_space=pltpu.VMEM),
        out_shape=jax.ShapeDtypeStruct((pair_count, full_width), jnp.bfloat16),
        scratch_shapes=[pltpu.VMEM((pair_count, full_width), jnp.bfloat16)],
        name="arrange",
    )(tile_order, amplitudes, amplitude_mask)
    placed = lax.all_to_all(ordered, "row", split_axis=1, concat_axis=0, tiled=True)

    def both_cores(mine, other):
        even, odd = jnp.where(core == 0, mine, other), jnp.where(core == 0, other, mine)
        return jnp.stack([even.reshape(32, 8, depth), odd.reshape(32, 8, depth)], axis=1).reshape(512, depth)

    over = send_col(placed, 2)
    near = both_cores(placed, send_col(placed, 1))

    def sent(rows):
        return jax.ShapeDtypeStruct((WIDTH_TILES * rows + 32, 128), jnp.int16)

    def floats(rows):
        return jax.ShapeDtypeStruct((rows, width), jnp.float32)

    call = Calls(placed)

    def kept(rows):
        return pltpu.VMEM((rows, width), jnp.float32)

    def left_rows(*rows):
        return [pltpu.VMEM((*rows, depth), jnp.bfloat16)]

    def exchange_both(outs, ahead=()):
        sends = []
        for k in range(2):
            p, q = outs[2 * k:2 * k + 2]
            if ahead:
                p, q, *_ = lax.optimization_barrier((p, q, *ahead[2 * k:2 * k + 2]))
            sends += [send(p, FORWARD[k]), send(q, BACKWARD[k])]
        return sends

    results = call(
        begin_kernel, [integral_mask, near], [sent(128)] * 4 + [pltpu.VMEM((depth, width), jnp.bfloat16)] * 2,
        left_rows(2, 256) + [pltpu.VMEM((integral_mask.shape[0], columns), jnp.float32)]
        + [pltpu.SemaphoreType.DMA((columns // FIRST_TILE,))] + scales(4), in_hbm=[integrals],
        limit=BEGIN_LIMIT,
    )
    n, weights = exchange_both(results[:4]), list(results[4:])
    over, _ = lax.optimization_barrier((over, call.last))
    far = both_cores(over, send_col(over, 1))

    f = exchange_both(call(far_kernel, weights + [far], [sent(128)] * 4, left_rows(256) + scales(4)), n)
    later = call(later_kernel, weights + [near, far, *n], [kept(256)] * 2, left_rows(256) + scales(4))
    d = []
    for k in range(2):
        p, q = call(pass_on_kernel, [later[k], *f[2 * k:2 * k + 2]], [sent(128)] * 2, scales(4))
        d += [send(p, FORWARD[k]), send(q, BACKWARD[k])]
    operands = [v for k in range(2) for v in (*n[2 * k:2 * k + 2], *f[2 * k:2 * k + 2])]
    own = call(own_kernel, weights + [near, far] + operands, [kept(256)] * 2, left_rows(256) + scales(8))

    def stage_one_of(kind):
        return [own[kind], *d[2 * kind:2 * kind + 2]]

    got = [None, None]
    for k in range(2):
        p, q = call(functools.partial(second_opposite_kernel, k), stage_one_of(k), [sent(32)] * 2, scales(4))
        got[k] = send(p, FORWARD[1 - k]), send(q, BACKWARD[1 - k])
    for k in range(2):
        p, q = call(
            functools.partial(second_neighbour_kernel, k), stage_one_of(k) + [*got[k]], [sent(64)] * 2, scales(6)
        )
        got[k] = send(p, FORWARD[1 - k]), send(q, BACKWARD[1 - k])
    for k in range(2):
        a, b, c, rest = call(
            functools.partial(spread_kernel, k), stage_one_of(k) + [*got[k]], [sent(16)] * 3 + [floats(16)],
            [pltpu.VMEM((64, TILE), jnp.float32)] + scales(7),
        )
        b, c = send_col(b, 2), lax.ppermute(c, ("row", "col"), DIAGONAL)
        got[k] = rest, send(a, ACROSS), b, c
    outs = []
    for k in range(2):
        outs.append(call(last_kernel, [*got[k]], [jax.ShapeDtypeStruct((16, width), jnp.bfloat16)] * 2, scales(3)))
    outs = [outs[k][part] for part in range(2) for k in range(2)]
    summed = jnp.concatenate(outs, axis=1).reshape(2, 8, 2 * columns)
    mine = lax.dynamic_index_in_dim(summed, core, 0, keepdims=False)
    other = send_col(lax.dynamic_index_in_dim(summed, 1 - core, 0, keepdims=False), 1)
    even, odd = jnp.where(core == 0, mine, other), jnp.where(core == 0, other, mine)
    near_pair = [even[:, :columns], odd[:, :columns]]
    far_pair = [even[:, columns:], odd[:, columns:]]
    first = [jnp.where(z_hi == 0, u, v) for u, v in zip(near_pair, far_pair)]
    last = [jnp.where(z_hi == 0, v, u) for u, v in zip(near_pair, far_pair)]
    return jnp.concatenate(first + last, axis=1)


def solution(mesh):
    in_specs = (
        P(("row", "col"), None),
        P(("row", "col"), None),
        P("row", "col"),
        P("row", "col"),
        P(),
    )
    out_specs = P(("row", "col"), None)
    return jax.shard_map(
        per_device, mesh=mesh, in_specs=in_specs, out_specs=out_specs, check_vma=False
    )
```

```python
import functools

import jax
import jax.numpy as jnp
from jax import lax
from jax.experimental import pallas as pl
from jax.experimental.pallas import tpu as pltpu
from jax.sharding import PartitionSpec as P

LEVELS = 32600.0
STEPS = 32.0
ROUNDER = 12582912.0
CODES = (32, 128)
VMEM_LIMIT = 12 * 1024 * 1024
BEGIN_LIMIT = 36 * 1024 * 1024
TILE = 896
FIRST_TILE = 896
WIDTH_TILES = 28


def shift(dz, dx, dy):
    pairs = []
    for index in range(32):
        z, x, y = index // 16, (index // 4) % 4, index % 4
        pairs.append((index, ((z + dz) % 2) * 16 + ((x + dx) % 4) * 4 + (y + dy) % 4))
    return pairs


FORWARD = (shift(0, 1, 0), shift(0, 0, 1))
BACKWARD = (shift(0, -1, 0), shift(0, 0, -1))
ACROSS = shift(1, 0, 0)
DIAGONAL = [(r * 4 + c, s * 4 + (c ^ 2)) for r, s in ACROSS for c in range(4)]


def send(value, pairs):
    return lax.ppermute(value, "row", pairs)


def send_col(value, step):
    return lax.ppermute(value, "col", [(c, c ^ step) for c in range(4)])


def quantised(value):
    rows, tile = value.shape
    largest = jnp.max(jnp.max(jnp.abs(value.reshape(rows // 8, 8, tile)), axis=0), axis=0, keepdims=True)
    code = jnp.ceil(jnp.log2(jnp.maximum(largest, 1e-30)) * STEPS)
    factor = jnp.exp2(code * (-1.0 / STEPS)) * LEVELS
    rounded = (value * factor + ROUNDER) - ROUNDER
    return rounded.astype(jnp.int32).astype(jnp.int16), code


def finish(out_ref, code_ref):
    out_ref[out_ref.shape[0] - 32:, :] = code_ref[...].astype(jnp.int32).astype(jnp.int16)


def encode(value, t, out_ref, code_ref):
    count, rows = value.shape[1] // 128, value.shape[0]
    coded, code = quantised(value)
    for i in range(count):
        at = t * count + i
        out_ref[pl.ds(pl.multiple_of(at * rows, 16), rows), :] = coded[:, i * 128:(i + 1) * 128]
        code_ref[pl.ds(at, 1), :] = code[:, i * 128:(i + 1) * 128]


def columns_of(t):
    return pl.ds(pl.multiple_of(t * TILE, 128), TILE)


def each_tile(width, unroll=1):
    return pl.loop(0, width // TILE, unroll=unroll)


def copy_rows(parts, left_ref, at, kind, first, z):
    first_stride, second_stride = (4, 1) if kind == 0 else (1, 4)
    for second in range(4):
        start = pl.multiple_of((z * 16 + second * second_stride + first * first_stride) * 16, 16)
        for part in parts:
            left_ref[at:at + 16, :] = part[pl.ds(start, 16), :]
            at += 16


def arrange_kernel(order, values, flags, out, kept):
    tiles = flags.shape[1]
    for t in range(tiles):
        at = slice(t * 128, (t + 1) * 128)
        kept[:, at] = values[:, at] * flags[:, t:t + 1].astype(jnp.float32).astype(jnp.bfloat16)
    for k in range(tiles):
        out[:, k * 128:(k + 1) * 128] = kept[:, pl.ds(pl.multiple_of(order[k] * 128, 128), 128)]


def clear(*code_refs):
    for code_ref in code_refs:
        code_ref[...] = jnp.zeros(CODES, jnp.float32)


def dot(left, right):
    return jnp.dot(left, right, preferred_element_type=jnp.float32)


def opposite_rows(pos, kind, a, left, at_p, at_q):
    first = (pos[1 + kind] + 2) % 4
    copy_rows((a,), left, at_p, kind, first, 0)
    copy_rows((a,), left, at_q, kind, first, 1)


def free_rows(pos, kind, a, left, at_p, at_q):
    copy_rows((a,), left, at_p, kind, (pos[1 + kind] + 1) % 4, 1)
    copy_rows((a,), left, at_q, kind, (pos[1 + kind] + 3) % 4, 0)


def begin_kernel(pos, b, m, a, p0, q0, p1, q1, w0, w1, left, wide, sems, *code_refs):
    tiles = w0.shape[1] // FIRST_TILE

    def copy(kind, t):
        w = (w0, w1)[kind]
        at = pl.ds(kind * tiles * FIRST_TILE + t * FIRST_TILE, FIRST_TILE)
        return pltpu.make_async_copy(b.at[:, at], w.at[:, pl.ds(t * FIRST_TILE, FIRST_TILE)], sems.at[kind * tiles + t])

    for t in range(tiles):
        for kind in range(2):
            copy(kind, t).start()
    for l in range(m.shape[1]):
        wide[:, l * 128:(l + 1) * 128] = jnp.broadcast_to(m[:, l:l + 1].astype(jnp.float32), (m.shape[0], 128))
    clear(*code_refs)
    for kind in range(2):
        opposite_rows(pos, kind, a, left.at[kind], 0, 128)
        free_rows(pos, kind, a, left.at[kind], 64, 192)
    for t in range(tiles):
        for kind, w, p, q in ((0, w0, p0, q0), (1, w1, p1, q1)):
            copy(kind, t).wait()
            at = slice(t * FIRST_TILE, (t + 1) * FIRST_TILE)
            flags = wide[:, (kind * tiles + t) * FIRST_TILE:(kind * tiles + t + 1) * FIRST_TILE].astype(jnp.bfloat16)
            for k in range(w.shape[0] // 128):
                rows = slice(k * 128, (k + 1) * 128)
                w[rows, at] = w[rows, at] * flags[k:k + 1, :]
            sums = dot(left[kind], w[:, at])
            encode(sums[:128], t, p, code_refs[2 * kind])
            encode(sums[128:], t, q, code_refs[2 * kind + 1])
    for ref, code_ref in zip((p0, q0, p1, q1), code_refs):
        finish(ref, code_ref)


def far_kernel(pos, w0, w1, a, p0, q0, p1, q1, left, *code_refs):
    clear(*code_refs)
    for kind, w, p, q in ((0, w0, p0, q0), (1, w1, p1, q1)):
        opposite_rows(pos, kind, a, left, 0, 128)
        free_rows(pos, kind, a, left, 64, 192)

        @each_tile(w.shape[1], 2)
        def _(t):
            sums = dot(left[...], w[:, columns_of(t)])
            encode(sums[:128], t, p, code_refs[2 * kind])
            encode(sums[128:], t, q, code_refs[2 * kind + 1])

        finish(p, code_refs[2 * kind])
        finish(q, code_refs[2 * kind + 1])


def own_kernel(pos, w0, w1, near, far, *refs):
    got, outs, left, factor_refs = refs[:8], refs[8:10], refs[10], refs[11:]
    for ref, factor in zip(got, factor_refs):
        read_factors(ref, factor)
    for kind, w, own in ((0, w0, outs[0]), (1, w1, outs[1])):
        for z in range(2):
            copy_rows((near, far), left, z * 128, kind, pos[1 + kind], z)

        @each_tile(w.shape[1], 2)
        def _(t):
            sums = dot(left[...], w[:, columns_of(t)])
            for z in range(2):
                parts = [
                    decode(got[4 * kind + at + 1 - z], factor_refs[4 * kind + at + 1 - z], t, 64, 64)
                    for at in (0, 2)
                ]
                value = sums[z * 128:z * 128 + 128] + mixed(*parts)
                own[z * 128:z * 128 + 128, columns_of(t)] = value


def mixed(near, far):
    return jnp.concatenate([part[at:at + 16] for at in range(0, 64, 16) for part in (near, far)], axis=0)


def read_factors(ref, factor_ref):
    codes = ref[ref.shape[0] - 32:, :].astype(jnp.int32).astype(jnp.float32)
    factor_ref[...] = jnp.exp2(codes * (1.0 / STEPS)) * (1.0 / LEVELS)


def decode(ref, factor_ref, t, start=0, size=None):
    count, rows = TILE // 128, (ref.shape[0] - 32) // WIDTH_TILES
    parts = []
    for i in range(count):
        at = t * count + i
        part = ref[pl.ds(pl.multiple_of(at * rows + start, 16), size or rows), :]
        parts.append(part.astype(jnp.int32).astype(jnp.float32) * factor_ref[pl.ds(at, 1), :])
    return jnp.concatenate(parts, axis=1)


def later_kernel(pos, w0, w1, near, far, *refs):
    got, outs, left, factor_refs = refs[:4], refs[4:6], refs[6], refs[7:]
    for ref, factor in zip(got, factor_refs):
        read_factors(ref, factor)
    for kind, w, out in ((0, w0, outs[0]), (1, w1, outs[1])):
        copy_rows((near, far), left, 0, kind, (pos[1 + kind] + 1) % 4, 0)
        copy_rows((near, far), left, 128, kind, (pos[1 + kind] + 3) % 4, 1)

        @each_tile(w.shape[1], 2)
        def _(t):
            sums = dot(left[...], w[:, columns_of(t)])
            for way in range(2):
                n = decode(got[2 * kind + way], factor_refs[2 * kind + way], t, 0, 64)
                out[way * 128:way * 128 + 128, columns_of(t)] = sums[way * 128:way * 128 + 128] + mixed(n, jnp.zeros_like(n))


def pass_on_kernel(pos, later, p, q, *refs):
    outs, factor_refs, code_refs = refs[:2], refs[2:4], refs[4:]
    clear(*code_refs)
    for ref, factor in zip((p, q), factor_refs):
        read_factors(ref, factor)

    @each_tile(later.shape[1], 2)
    def _(t):
        for way, ref in enumerate((p, q)):
            f = decode(ref, factor_refs[way], t, 0, 64)
            value = later[way * 128:way * 128 + 128, columns_of(t)] + mixed(jnp.zeros_like(f), f)
            encode(value, t, outs[way], code_refs[way])

    for way in range(2):
        finish(outs[way], code_refs[way])


def stage_one(refs, factor_refs, second, t):
    own, *got = refs
    return [
        own[pl.ds(pl.multiple_of(z * 128 + second * 32, 32), 32), columns_of(t)] + decode(got[z], factor_refs[z], t, second * 32, 32)
        for z in range(2)
    ]


def second_opposite_kernel(kind, pos, *refs):
    some, outs, factor_refs, code_refs = refs[:3], refs[3:5], refs[5:7], refs[7:]
    clear(*code_refs)
    for ref, factor in zip(some[1:], factor_refs):
        read_factors(ref, factor)

    @each_tile(some[0].shape[1], 2)
    def _(t):
        sums = stage_one(some, factor_refs, (pos[2 - kind] + 2) % 4, t)
        for z in range(2):
            encode(sums[z], t, outs[z], code_refs[z])

    for z in range(2):
        finish(outs[z], code_refs[z])


def second_neighbour_kernel(kind, pos, *refs):
    some, got, outs, factor_refs, code_refs = refs[:3], refs[3:5], refs[5:7], refs[7:11], refs[11:]
    clear(*code_refs)
    for ref, factor in zip(refs[1:5], factor_refs):
        read_factors(ref, factor)

    @each_tile(some[0].shape[1], 2)
    def _(t):
        for way in range(2):
            sums = stage_one(some, factor_refs[:2], (pos[2 - kind] + (1 if way == 0 else 3)) % 4, t)
            sums[way] = sums[way] + decode(got[way], factor_refs[2 + way], t)
            encode(jnp.concatenate(sums, axis=0), t, outs[way], code_refs[way])

    for way in range(2):
        finish(outs[way], code_refs[way])


def spread_kernel(kind, pos, *refs):
    some, got, outs, sums, factor_refs, code_refs = refs[:3], refs[3:5], refs[5:9], refs[9], refs[10:14], refs[14:]
    clear(*code_refs)
    z = pos[0]
    for ref, factor in zip(refs[1:5], factor_refs):
        read_factors(ref, factor)

    def rows(h, far):
        return sums[pl.ds(pl.multiple_of(h * 32 + far * 16, 16), 16), :]

    @each_tile(some[0].shape[1], 2)
    def _(t):
        value = jnp.concatenate(stage_one(some, factor_refs[:2], pos[2 - kind], t), axis=0)
        sums[...] = value + decode(got[0], factor_refs[2], t) + decode(got[1], factor_refs[3], t)
        for at, (h, far) in enumerate(((1 - z, 0), (z, 1), (1 - z, 1))):
            encode(rows(h, far), t, outs[at], code_refs[at])
        outs[3][:, columns_of(t)] = rows(z, 0)

    for at in range(3):
        finish(outs[at], code_refs[at])


def last_kernel(pos, rest, a, b, c, near, far, f0, f1, f2):
    for ref, factor in ((a, f0), (b, f1), (c, f2)):
        read_factors(ref, factor)

    @each_tile(rest.shape[1], 2)
    def _(t):
        at = columns_of(t)
        near[:, at] = (rest[:, at] + decode(a, f0, t)).astype(jnp.bfloat16)
        far[:, at] = (decode(b, f1, t) + decode(c, f2, t)).astype(jnp.bfloat16)


def assemble_kernel(mine, other, out):
    col = lax.axis_index("col")
    columns = mine.shape[1] // 2
    for far in range(2):
        for step, ref in enumerate((mine, other)):
            block = (col + 2 * far) % 4 if step == 0 else (col + 1 - 2 * (col % 2) + 2 * far) % 4
            at = pl.multiple_of(block * columns, 128)
            out[:, pl.ds(at, columns)] = ref[:, far * columns:(far + 1) * columns]


COST = pl.CostEstimate(flops=1000, bytes_accessed=1000, transcendentals=0)


def position():
    row = lax.axis_index("row")
    return row // 16, (row // 4) % 4, row % 4


class Calls:
    def __init__(self, first):
        self.last = first

    def __call__(self, kernel, values, outs, scratch=(), after=(), in_hbm=(), limit=VMEM_LIMIT):
        after = [self.last, *after]
        skipped = len(after)
        name = kernel.func.__name__ if isinstance(kernel, functools.partial) else kernel.__name__
        vmem = pl.BlockSpec(memory_space=pltpu.VMEM)
        results = pl.pallas_call(
            lambda *refs: kernel(position(), *refs[skipped:]),
            in_specs=[pl.BlockSpec(memory_space=pl.ANY)] * skipped
            + [pl.BlockSpec(memory_space=pltpu.HBM)] * len(in_hbm) + [vmem] * len(values),
            out_specs=[vmem] * len(outs),
            out_shape=outs,
            scratch_shapes=list(scratch),
            compiler_params=pltpu.CompilerParams(vmem_limit_bytes=limit),
            cost_estimate=COST,
            name=name,
        )(*after, *in_hbm, *values)
        self.last = results[0]
        return results


def scales(count):
    return [pltpu.VMEM(CODES, jnp.float32)] * count


def per_device(amplitudes, amplitude_mask, integrals, integral_mask, tile_order):
    pair_count, full_width = amplitudes.shape
    depth, columns = integrals.shape
    width = columns // 2
    col = lax.axis_index("col")
    core, z_hi = col % 2, col // 2

    ordered = pl.pallas_call(
        arrange_kernel,
        in_specs=[pl.BlockSpec(memory_space=pltpu.SMEM)] + [pl.BlockSpec(memory_space=pltpu.VMEM)] * 2,
        out_specs=pl.BlockSpec(memory_space=pltpu.VMEM),
        out_shape=jax.ShapeDtypeStruct((pair_count, full_width), jnp.bfloat16),
        scratch_shapes=[pltpu.VMEM((pair_count, full_width), jnp.bfloat16)],
        name="arrange",
    )(tile_order, amplitudes, amplitude_mask)
    placed = lax.all_to_all(ordered, "row", split_axis=1, concat_axis=0, tiled=True)

    def both_cores(mine, other):
        even, odd = jnp.where(core == 0, mine, other), jnp.where(core == 0, other, mine)
        return jnp.stack([even.reshape(32, 8, depth), odd.reshape(32, 8, depth)], axis=1).reshape(512, depth)

    over = send_col(placed, 2)
    near = both_cores(placed, send_col(placed, 1))

    def sent(rows):
        return jax.ShapeDtypeStruct((WIDTH_TILES * rows + 32, 128), jnp.int16)

    def floats(rows):
        return jax.ShapeDtypeStruct((rows, width), jnp.float32)

    call = Calls(placed)

    def kept(rows):
        return pltpu.VMEM((rows, width), jnp.float32)

    def left_rows(*rows):
        return [pltpu.VMEM((*rows, depth), jnp.bfloat16)]

    def exchange_both(outs, ahead=()):
        sends = []
        for k in range(2):
            p, q = outs[2 * k:2 * k + 2]
            if ahead:
                p, q, *_ = lax.optimization_barrier((p, q, *ahead[2 * k:2 * k + 2]))
            sends += [send(p, FORWARD[k]), send(q, BACKWARD[k])]
        return sends

    results = call(
        begin_kernel, [integral_mask, near], [sent(128)] * 4 + [pltpu.VMEM((depth, width), jnp.bfloat16)] * 2,
        left_rows(2, 256) + [pltpu.VMEM((integral_mask.shape[0], columns), jnp.float32)]
        + [pltpu.SemaphoreType.DMA((columns // FIRST_TILE,))] + scales(4), in_hbm=[integrals],
        limit=BEGIN_LIMIT,
    )
    n, weights = exchange_both(results[:4]), list(results[4:])
    over, _ = lax.optimization_barrier((over, call.last))
    far = both_cores(over, send_col(over, 1))

    f = exchange_both(call(far_kernel, weights + [far], [sent(128)] * 4, left_rows(256) + scales(4)), n)
    later = call(later_kernel, weights + [near, far, *n], [kept(256)] * 2, left_rows(256) + scales(4))
    d = []
    for k in range(2):
        p, q = call(pass_on_kernel, [later[k], *f[2 * k:2 * k + 2]], [sent(128)] * 2, scales(4))
        d += [send(p, FORWARD[k]), send(q, BACKWARD[k])]
    operands = [v for k in range(2) for v in (*n[2 * k:2 * k + 2], *f[2 * k:2 * k + 2])]
    own = call(own_kernel, weights + [near, far] + operands, [kept(256)] * 2, left_rows(256) + scales(8))

    def stage_one_of(kind):
        return [own[kind], *d[2 * kind:2 * kind + 2]]

    got = [None, None]
    for k in range(2):
        p, q = call(functools.partial(second_opposite_kernel, k), stage_one_of(k), [sent(32)] * 2, scales(4))
        got[k] = send(p, FORWARD[1 - k]), send(q, BACKWARD[1 - k])
    for k in range(2):
        p, q = call(
            functools.partial(second_neighbour_kernel, k), stage_one_of(k) + [*got[k]], [sent(64)] * 2, scales(6)
        )
        got[k] = send(p, FORWARD[1 - k]), send(q, BACKWARD[1 - k])
    for k in range(2):
        a, b, c, rest = call(
            functools.partial(spread_kernel, k), stage_one_of(k) + [*got[k]], [sent(16)] * 3 + [floats(16)],
            [pltpu.VMEM((64, TILE), jnp.float32)] + scales(7),
        )
        b, c = send_col(b, 2), lax.ppermute(c, ("row", "col"), DIAGONAL)
        got[k] = rest, send(a, ACROSS), b, c
    outs = []
    for k in range(2):
        outs.append(call(last_kernel, [*got[k]], [jax.ShapeDtypeStruct((16, width), jnp.bfloat16)] * 2, scales(3)))
    outs = [outs[k][part] for part in range(2) for k in range(2)]
    summed = jnp.concatenate(outs, axis=1).reshape(2, 8, 2 * columns)
    mine = lax.dynamic_index_in_dim(summed, core, 0, keepdims=False)
    other = send_col(lax.dynamic_index_in_dim(summed, 1 - core, 0, keepdims=False), 1)
    return pl.pallas_call(
        assemble_kernel,
        in_specs=[pl.BlockSpec(memory_space=pltpu.VMEM)] * 2,
        out_specs=pl.BlockSpec(memory_space=pltpu.VMEM),
        out_shape=jax.ShapeDtypeStruct((pair_count, full_width), jnp.bfloat16),
        compiler_params=pltpu.CompilerParams(vmem_limit_bytes=VMEM_LIMIT),
        name="assemble",
    )(mine, other)


def solution(mesh):
    in_specs = (
        P(("row", "col"), None),
        P(("row", "col"), None),
        P("row", "col"),
        P("row", "col"),
        P(),
    )
    out_specs = P(("row", "col"), None)
    return jax.shard_map(
        per_device, mesh=mesh, in_specs=in_specs, out_specs=out_specs, check_vma=False
    )
```
